512 devices in a mesh: grp: 64 (over z_hi, y, x), intra: 8 (over z_lo, core).
Axes of the slice: x: 4, y: 4, z: 16 (z_hi: 4, z_lo: 4; z = z_hi * 4 + z_lo), core: 2. Of those that a mesh axis runs over, the one named last changes fastest.
Arguments:
- activations: bfloat16 [20480, 14848], P('grp', 'intra'), may hold values from -400 to 400
- norm_gain: bfloat16 [14848], P(('intra', 'grp')), may hold values from 0.099609375 to 1.8984375
- norm_bias: bfloat16 [14848], P(('intra', 'grp')), may hold values from -3 to 3
- kv_weight: bfloat16 [14848, 512], P(('intra', 'grp')), may hold values from -0.046875 to 0.046875
- kv_cotangent: bfloat16 [20480, 512], P(('grp', 'intra')), may hold values from -6 to 6
Outputs:
- projected: bfloat16 [20480, 512], P(('grp', 'intra'))
- input_grad: bfloat16 [20480, 14848], P('grp', 'intra')
- weight_grad: float32 [14848, 512], P(('intra', 'grp'))
- gain_grad: float32 [14848], P(('intra', 'grp'))
- bias_grad: float32 [14848], P(('intra', 'grp'))
The draws below stay inside these ranges and needn't reach their ends.
All inputs are finite; a program needn't handle non-finite values.
Results may differ from the reference program's by a relative error of at most 0.017.
Values may be sent and summed in bfloat16 or wider, within the bound.
A program may use at most 64 MiB of HBM per device.

```python
import jax
import jax.numpy as jnp
from jax import lax

D = 14848
COLS = 512
TOKG = 320
TOKENS = 20480
N_GRP = 64
N_INTRA = 8


def draw_activations(key, part):
    key = jax.random.fold_in(key, 11)
    key_rows, key_cols, key_base = jax.random.split(key, 3)
    row_scale = jnp.exp(jax.random.uniform(key_rows, (TOKENS, 1), minval=0.0, maxval=2.3))
    position = jnp.arange(D).astype(jnp.float32) / D
    col_scale = jnp.exp(jax.random.uniform(key_cols, (1, D), minval=-1.15, maxval=1.15)) * (0.5 + 1.5 * position)[None, :]
    base = jnp.clip(jax.random.normal(key_base, (TOKENS, D)), -6.0, 6.0)
    return (base * row_scale * col_scale).astype(jnp.bfloat16)


def steps_of(own_key, extent, cuts, low, largest):
    def one(axis_at, shards_of):
        heights = jax.random.uniform(jax.random.fold_in(jax.random.fold_in(own_key, 6), axis_at), (shards_of,), jnp.float32, low / len(cuts), largest / len(cuts))
        return jnp.repeat(jnp.exp(heights), extent[axis_at] // shards_of).reshape((-1,) + (1,) * (len(extent) - axis_at - 1))

    level = one(*cuts[0])
    for cut in cuts[1:]:
        level = level * one(*cut)
    return level


def normal_values(stream_key, extent, deviation, limit, cuts=(), dtype=jnp.bfloat16):
    values = deviation * jax.random.normal(stream_key, extent, jnp.float32)
    if cuts:
        values = values * steps_of(stream_key, extent, cuts, -0.22, 0.18)
    return jnp.clip(values, -limit, limit).astype(dtype)


def setup_inputs(seed: int = 0) -> dict:
    seeds = jax.random.split(jax.random.key(seed), 6)
    activations = draw_activations(jax.random.fold_in(seeds[5], 71), 0)
    norm_gain = jnp.clip(1.0 + 0.18 * jax.random.normal(seeds[1], (D,), jnp.float32), 0.099609375, 1.8984375).astype(jnp.bfloat16)
    norm_bias = normal_values(seeds[2], (D,), 0.5, 3.0, ((0, 512),))
    kv_weight = normal_values(seeds[3], (D, COLS), D ** -0.5, 0.046875, ((0, 512),))
    kv_cotangent = normal_values(seeds[4], (TOKENS, COLS), 1.0, 6.0, ((0, 512),))
    return {"activations": activations, "norm_gain": norm_gain, "norm_bias": norm_bias, "kv_weight": kv_weight, "kv_cotangent": kv_cotangent}


epsilon = 1e-05

def reference(activations, norm_gain, norm_bias, kv_weight, kv_cotangent):
    norm_scale = norm_gain.astype(jnp.float32)
    offset = norm_bias.astype(jnp.float32)
    block_rows = D // N_INTRA
    weight_blocks = kv_weight.reshape(N_INTRA, block_rows, COLS).astype(jnp.float32)

    def one_group(running, pieces):
        rows_in, rows_cot = pieces
        floats = rows_in.astype(jnp.float32)
        average = lax.optimization_barrier(jnp.mean(floats, axis=1, keepdims=True))
        spread = lax.optimization_barrier(jnp.mean(floats * floats, axis=1, keepdims=True)) - average * average
        inverse = lax.rsqrt(spread + epsilon)
        centred = (floats - average) * inverse
        normed = (centred * norm_scale + offset).astype(jnp.bfloat16)
        partial_value = jnp.einsum('tjb,jbc->jtc', normed.reshape(TOKG, N_INTRA, block_rows).astype(jnp.float32), weight_blocks)
        rounded = lax.optimization_barrier(partial_value.astype(jnp.bfloat16)).astype(jnp.float32)
        projected = lax.optimization_barrier(jnp.sum(rounded, axis=0)).astype(jnp.bfloat16)
        normed_grad = jnp.dot(rows_cot, kv_weight.T, preferred_element_type=jnp.float32)
        scaled = normed_grad * norm_scale
        grad_mean = lax.optimization_barrier(jnp.mean(scaled, axis=1, keepdims=True))
        cross_mean = lax.optimization_barrier(jnp.mean(scaled * centred, axis=1, keepdims=True))
        input_grad = (inverse * (scaled - grad_mean - centred * cross_mean)).astype(jnp.bfloat16)
        weight_acc, gain_acc, bias_acc = running
        weight_acc = weight_acc + jnp.dot(normed.T, rows_cot, preferred_element_type=jnp.float32)
        gain_acc = gain_acc + lax.optimization_barrier(jnp.sum(normed_grad * centred, axis=0))
        bias_acc = bias_acc + lax.optimization_barrier(jnp.sum(normed_grad, axis=0))
        return ((weight_acc, gain_acc, bias_acc), (projected, input_grad))
    initial = (jnp.zeros((D, COLS), jnp.float32), jnp.zeros((D,), jnp.float32), jnp.zeros((D,), jnp.float32))
    totals, outputs = lax.scan(one_group, initial, (activations.reshape(N_GRP, TOKG, D), kv_cotangent.reshape(N_GRP, TOKG, COLS)))
    weight_grad, gain_grad, bias_grad = totals
    projected, input_grad = outputs
    return (projected.reshape(TOKENS, COLS), input_grad.reshape(TOKENS, D), weight_grad, gain_grad, bias_grad)
```

```python
import jax
import jax.numpy as jnp
from jax import lax
from jax.experimental import pallas as pl
from jax.experimental.pallas import tpu as pltpu
from jax.sharding import PartitionSpec as P

epsilon = 1e-05
F32, BF16 = jnp.float32, jnp.bfloat16
MESH = pl.DeviceIdType.MESH

T = 320
F = 1856
C = 512
H = 256
R = 29
SLOT = 32
OWN = 40
NI = 8
D = F * NI
COPIES = 80


def pack(v):
    tail = jnp.concatenate([v[32:40, :H], v[32:40, H:]], axis=0)
    return jnp.concatenate([v[0:16], v[16:32], tail], axis=1)


def unpack(v):
    tail = jnp.concatenate([v[0:8, 1024:], v[8:16, 1024:]], axis=1)
    return jnp.concatenate([v[:, :C], v[:, C:1024], tail], axis=0)


def iota(shape, dim):
    return lax.broadcasted_iota(jnp.int32, shape, dim)


def kernel(
    x_hbm, w_ref, gain_ref, bias_ref, cot_ref,
    proj_ref, ig_hbm, wg_ref, gg_ref, bg_ref,
    xv, cv, igv, wfull, spread_m, squeeze_m, cot32, cotb, cotg, m32, wc, part32,
    gath, scat, land1, land2, scat2, land3, land4, scat3, land5, land6,
    st, stats1, stats2, cols, cols2, pown, pland,
    sends, recvs, local,
):
    grp, me = lax.axis_index("grp"), lax.axis_index("intra")
    z, y, x = grp // 16, (grp // 4) % 4, grp % 4
    core = me % 2

    def up(v, by):
        return (v + by) % 4

    def to_grp(axis, by):
        if axis == "z":
            return {"grp": up(z, by) * 16 + y * 4 + x, "intra": me}
        if axis == "y":
            return {"grp": z * 16 + up(y, by) * 4 + x, "intra": me}
        return {"grp": z * 16 + y * 4 + up(x, by), "intra": me}

    count = [0]

    def remote(src, dst, device):
        k = count[0]
        count[0] += 1
        return pltpu.make_async_remote_copy(
            src_ref=src, dst_ref=dst, send_sem=sends.at[k], recv_sem=recvs.at[k],
            device_id={"grp": device["grp"], "intra": device["intra"]}, device_id_type=MESH,
        )

    started = []

    def start(copies):
        for c in copies:
            c.start()
            started.append(c)
        return copies

    def arrive(copies):
        for c in copies:
            c.wait_recv()

    x_copy = pltpu.make_async_copy(x_hbm, xv, local.at[0])
    x_copy.start()

    peers = [to_grp(a, by) for a in "zyx" for by in (1, 3)]
    peers += [{"grp": grp, "intra": (me + d) % NI} for d in range(1, NI)]
    barrier = pltpu.get_barrier_semaphore()
    for peer in peers:
        pl.semaphore_signal(barrier, inc=1, device_id=peer, device_id_type=MESH)

    diagonal = iota((SLOT, R), 0) == iota((SLOT, R), 1)

    def column(ref):
        row = ref[...].astype(F32)
        return jnp.sum(jnp.where(diagonal, row, 0.0), axis=1, keepdims=True)

    gain, bias = column(gain_ref), column(bias_ref)
    wfull[...] = jnp.zeros_like(wfull)
    wfull[0:R, :] = w_ref[...].astype(F32)
    weight = wfull[...]
    product = jnp.sum(weight * bias, axis=0, keepdims=True)
    high = product.astype(BF16).astype(F32)
    row = iota((SLOT, C), 0)
    slot = jnp.where(row == R, high, jnp.where(row == R + 1, product - high, weight * gain)).astype(BF16)
    gath[0, z, y, x] = slot[:, :H]
    gath[1, z, y, x] = slot[:, H:]
    cotg[me] = pack(cot_ref[...].astype(F32)).astype(BF16)

    pl.semaphore_wait(barrier, len(peers))

    gz1 = start([
        remote(gath.at[:, z, y, x], gath.at[:, z, y, x], to_grp("z", 1)),
        remote(gath.at[:, z, y, x], gath.at[:, z, y, x], to_grp("z", 3)),
    ])
    mate = {"grp": grp, "intra": me + 1 - 2 * core}
    ct1 = start([remote(cotg.at[me], cotg.at[me], mate)])
    ct1 += start([
        remote(cotg.at[me], cotg.at[me], {"grp": grp, "intra": (me + d) % NI}) for d in (2, 6, 4)
    ])

    a, b = iota((H, 8 * R), 0), iota((H, 8 * R), 1)
    spread_m[...] = jnp.where(((a & 31) < R) & (b == R * (a >> 5) + (a & 31)), 1.0, 0.0).astype(BF16)
    a, b = iota((240, H), 0), iota((240, H), 1)
    within = b & 31
    hit = (within < R) & ((a == R * (b >> 5) + within) | (a == 233))
    hit = hit | ((within >= R) & (within < R + 2) & (a == 232))
    squeeze_m[...] = jnp.where(hit, 1.0, 0.0).astype(BF16)

    x_copy.wait()
    st[...] = jnp.zeros_like(st)
    lane = iota((64, 128), 1)
    for r in range(0, T, 64):
        v = xv[r:r + 64, :].astype(F32)
        s1 = jnp.sum(v, axis=1, keepdims=True)
        s2 = jnp.sum(v * v, axis=1, keepdims=True)
        st[r:r + 64, :] = jnp.where(lane == 0, s1, jnp.where(lane == 1, s2, 0.0))
    stats1[me] = st[...].T[0:2, :]
    ex1 = start([
        remote(stats1.at[me], stats1.at[me], {"grp": grp, "intra": (me + d) % NI}) for d in range(1, NI)
    ])

    arrive(gz1)
    gz2 = start([
        remote(gath.at[0, up(z, 3), y, x], gath.at[0, up(z, 3), y, x], to_grp("z", 1)),
        remote(gath.at[1, up(z, 1), y, x], gath.at[1, up(z, 1), y, x], to_grp("z", 3)),
    ])
    arrive(ct1)
    ct2 = start([
        remote(cotg.at[(me + d) % NI], cotg.at[(me + d) % NI], mate) for d in (6, 2, 4)
    ])

    def stage(views, axes):
        first = []
        for h in (0, 1):
            p = {"y": y, "x": x}[axes[h]]
            first += [
                remote(views[h](p, 0), views[h](p, 0), to_grp(axes[h], 1)),
                remote(views[h](p, 0), views[h](p, 0), to_grp(axes[h], 3)),
            ]
        return start(first)

    def forward(views, axes, first):
        second = []
        for h in (0, 1):
            p = {"y": y, "x": x}[axes[h]]
            arrive(first[2 * h:2 * h + 2])
            second += start([
                remote(views[h](up(p, 3), 1), views[h](up(p, 3), 1), to_grp(axes[h], 1)),
                remote(views[h](up(p, 1), 2), views[h](up(p, 1), 2), to_grp(axes[h], 3)),
            ])
        return second

    part_of = (slice(None), slice(0, 2), slice(2, 4))
    g2 = (
        lambda p, part: gath.at[0, part_of[part], p, x],
        lambda p, part: gath.at[1, part_of[part], y, p],
    )
    g3 = (
        lambda p, part: gath.at[0, part_of[part], :, p],
        lambda p, part: gath.at[1, part_of[part], p, :],
    )

    arrive(gz2)
    s2a = stage(g2, "yx")

    arrive(ex1)
    sums = jnp.sum(stats1[...], axis=0)
    average = sums[0:1] / D
    inverse = lax.rsqrt(sums[1:2] / D - average * average + epsilon)
    pick = iota((128, 384), 0)
    cols[...] = jnp.where(pick == 0, average, jnp.where(pick == 1, inverse, 0.0)).T
    for r in range(0, T, 64):
        v = xv[r:r + 64, :].astype(F32)
        cv[r:r + 64, :] = ((v - cols[r:r + 64, 0:1]) * cols[r:r + 64, 1:2]).astype(BF16)

    s2b = forward(g2, "yx", s2a)

    arrive(ct2)
    for s in range(NI):
        cot32[OWN * s:OWN * s + OWN, :] = unpack(cotg[s].astype(F32))
    cotb[...] = cot32[...].astype(BF16)
    cot_sum = jnp.sum(cot32[...], axis=0, keepdims=True)

    arrive(s2b)
    s3a = stage(g3, "xy")

    for f in range(0, F, 256):
        g = min(f + 256, F)
        m32[f:g, :] = lax.dot_general(
            cv[:, f:g], cotb[...], (((0,), (0,)), ((), ())), preferred_element_type=F32
        )
    spare = (iota((H, C), 0) & 31) == R
    for j in range(8):
        rows = m32[8 * R * j:8 * R * (j + 1), :].astype(BF16)
        wide = jnp.dot(spread_m[...], rows, preferred_element_type=F32)
        wide = jnp.where(spare, cot_sum, wide).astype(BF16)
        at = 2 * (j % 2)
        scat[0, j // 2, at:at + 2] = wide[:, :H].reshape(2, 4, SLOT, H)
        scat[1, j // 2, at:at + 2] = wide[:, H:].reshape(2, 4, SLOT, H)

    def sa(h, p, part):
        return scat.at[0, part_of[part], :, p] if h == 0 else scat.at[1, part_of[part], p, :]

    def sb(h, p, part):
        return scat2.at[h, part_of[part], p]

    def scatter_one(view, land, axes):
        copies = []
        for h in (0, 1):
            p = {"y": y, "x": x}[axes[h]]
            copies += [
                remote(view(h, up(p, 2), 1), land.at[h, 0], to_grp(axes[h], 1)),
                remote(view(h, up(p, 2), 2), land.at[h, 1], to_grp(axes[h], 3)),
            ]
        return start(copies)

    def scatter_two(view, land, out, axes, copies):
        second = []
        for h in (0, 1):
            p = {"y": y, "x": x}[axes[h]]
            arrive(copies[2 * h:2 * h + 2])
            for side, by in ((0, 1), (1, 3)):
                ref = view(h, up(p, by), 1 + side)
                ref[...] = (ref[...].astype(F32) + land[h, side].astype(F32)).astype(BF16)
                second += start([remote(view(h, up(p, by), 0), out.at[h, side], to_grp(axes[h], by))])
        return second

    ra = scatter_one(sa, land1, "xy")
    s3b = forward(g3, "xy", s3a)
    rb = scatter_two(sa, land1, land2, "xy", ra)
    arrive(s3b)

    extra = [jnp.zeros((8, H), F32), jnp.zeros((8, H), F32)]
    for h in (0, 1):
        for j in range(4):
            block = gath[h, j].reshape(16 * SLOT, H)
            p0 = jnp.dot(squeeze_m[...], block[:H], preferred_element_type=F32)
            p1 = jnp.dot(squeeze_m[...], block[H:], preferred_element_type=F32)
            rows = jnp.concatenate([p0[:8 * R], p1[:8 * R]], axis=0)
            wc[16 * R * j:16 * R * (j + 1), H * h:H * (h + 1)] = rows.astype(BF16)
            extra[h] = extra[h] + p0[8 * R:] + p1[8 * R:]
    extra = jnp.concatenate(extra, axis=1)
    bias_row, weight_row = extra[0:1], extra[1:2]

    part32[...] = jnp.dot(cv[...], wc[...], preferred_element_type=F32)
    cross = jnp.sum(cot32[...] * part32[...], axis=1, keepdims=True)
    plain = jnp.sum(cot32[...] * weight_row, axis=1, keepdims=True)
    lane = iota((T, 128), 1)
    st[0:T, :] = jnp.where(lane == 0, plain, jnp.where(lane == 1, cross, 0.0))
    stats2[me] = st[...].T[0:2, :]
    ex2 = start([
        remote(stats2.at[me], stats2.at[me], {"grp": grp, "intra": (me + d) % NI}) for d in range(1, NI)
    ])
    for s in range(NI):
        pown[s] = pack(part32[OWN * s:OWN * s + OWN, :] + bias_row).astype(BF16)
    exp = start([
        remote(pown.at[(me + d) % NI], pland.at[d - 1], {"grp": grp, "intra": (me + d) % NI})
        for d in range(1, NI)
    ])

    def scatter_three(view, out, axes, copies, store):
        for h in (0, 1):
            p = {"y": y, "x": x}[axes[h]]
            arrive(copies[2 * h:2 * h + 2])
            total = view(h, p, 0)[...].astype(F32) + out[h, 0].astype(F32) + out[h, 1].astype(F32)
            store(h, total.astype(BF16))

    def store2(h, value):
        scat2[h] = value

    def store3(h, value):
        scat3[h] = value

    scatter_three(sa, land2, "xy", rb, store2)
    rc = scatter_one(sb, land3, "yx")

    arrive(ex2)
    means = jnp.sum(stats2[...], axis=0) / D
    cols2[...] = jnp.where(pick == 0, means[0:1], jnp.where(pick == 1, means[1:2], 0.0)).T

    def input_part(f):
        g = min(f + 256, F)
        scaled = lax.dot_general(
            cotb[...], wc[f:g, :], (((1,), (1,)), ((), ())), preferred_element_type=F32
        )
        centred = (xv[:, f:g].astype(F32) - cols[0:T, 0:1]) * cols[0:T, 1:2]
        value = cols[0:T, 1:2] * (scaled - cols2[0:T, 0:1] - centred * cols2[0:T, 1:2])
        igv[:, f:g] = value.astype(BF16)

    for f in range(0, 1024, 256):
        input_part(f)
    rd = scatter_two(sb, land3, land4, "yx", rc)
    for f in range(1024, F, 256):
        input_part(f)
    ig_copy = pltpu.make_async_copy(igv, ig_hbm, local.at[1])
    ig_copy.start()

    scatter_three(sb, land4, "yx", rd, store3)
    re = start([
        remote(scat3.at[0, up(z, 2)], land5.at[0], to_grp("z", 1)),
        remote(scat3.at[1, up(z, 2)], land5.at[1], to_grp("z", 3)),
    ])

    arrive(exp)
    total = pown[me].astype(F32)
    for d in range(NI - 1):
        total = total + pland[d].astype(F32)
    proj_ref[...] = unpack(total).astype(BF16)

    arrive(re)
    scat3[0, up(z, 1)] = (scat3[0, up(z, 1)].astype(F32) + land5[0].astype(F32)).astype(BF16)
    scat3[1, up(z, 3)] = (scat3[1, up(z, 3)].astype(F32) + land5[1].astype(F32)).astype(BF16)
    rf = start([
        remote(scat3.at[:, up(z, 1)], land6.at[0], to_grp("z", 1)),
        remote(scat3.at[:, up(z, 3)], land6.at[1], to_grp("z", 3)),
    ])
    arrive(rf)
    halves = [
        scat3[h, z].astype(F32) + land6[0, h].astype(F32) + land6[1, h].astype(F32) for h in (0, 1)
    ]
    total = jnp.concatenate(halves, axis=1)
    sum_row = total[R:R + 1]
    weight = wfull[...]
    wg_ref[...] = (total * gain + bias * sum_row)[:R]

    def as_row(v):
        return jnp.sum(jnp.where(diagonal, v, 0.0), axis=0, keepdims=True)

    gg_ref[...] = as_row(jnp.sum(weight * total, axis=1, keepdims=True))
    bg_ref[...] = as_row(jnp.sum(weight * sum_row, axis=1, keepdims=True))

    for c in started:
        c.wait_send()
    ig_copy.wait()


def shards(activations, norm_gain, norm_bias, kv_weight, kv_cotangent):
    vmem = pl.BlockSpec(memory_space=pltpu.VMEM)
    hbm = pl.BlockSpec(memory_space=pl.ANY)

    def v16(*shape):
        return pltpu.VMEM(shape, BF16)

    def v32(*shape):
        return pltpu.VMEM(shape, F32)

    projected, input_grad, weight_grad, gain_grad, bias_grad = pl.pallas_call(
        kernel,
        out_shape=(
            jax.ShapeDtypeStruct((OWN, C), BF16),
            jax.ShapeDtypeStruct((T, F), BF16),
            jax.ShapeDtypeStruct((R, C), F32),
            jax.ShapeDtypeStruct((1, R), F32),
            jax.ShapeDtypeStruct((1, R), F32),
        ),
        in_specs=[hbm, vmem, vmem, vmem, vmem],
        out_specs=(vmem, hbm, vmem, vmem, vmem),
        scratch_shapes=[
            v16(T, F), v16(T, F), v16(T, F),
            v32(SLOT, C), v16(H, 8 * R), v16(240, H),
            v32(T, C), v16(T, C), v16(NI, 16, 1280), v32(F, C),
            v16(F, C), v32(T, C),
            v16(2, 4, 4, 4, SLOT, H), v16(2, 4, 4, 4, SLOT, H),
            v16(2, 2, 2, 4, SLOT, H), v16(2, 2, 4, 4, SLOT, H),
            v16(2, 4, 4, SLOT, H), v16(2, 2, 2, SLOT, H), v16(2, 2, 4, SLOT, H),
            v16(2, 4, SLOT, H), v16(2, SLOT, H), v16(2, 2, SLOT, H),
            v32(384, 128), v32(NI, 2, 384), v32(NI, 2, 384),
            v32(384, 128), v32(384, 128),
            v16(NI, 16, 1280), v16(NI - 1, 16, 1280),
            pltpu.SemaphoreType.DMA((COPIES,)),
            pltpu.SemaphoreType.DMA((COPIES,)),
            pltpu.SemaphoreType.DMA((2,)),
        ],
        compiler_params=pltpu.CompilerParams(
            collective_id=0, has_side_effects=True, vmem_limit_bytes=48 * 1024 * 1024
        ),
    )(activations, kv_weight, norm_gain.reshape(1, R), norm_bias.reshape(1, R), kv_cotangent)
    return projected, input_grad, weight_grad, gain_grad.reshape(R), bias_grad.reshape(R)


def solution(mesh):
    return jax.shard_map(
        shards,
        mesh=mesh,
        in_specs=(
            P("grp", "intra"),
            P(("intra", "grp")),
            P(("intra", "grp")),
            P(("intra", "grp"), None),
            P(("grp", "intra"), None),
        ),
        out_specs=(
            P(("grp", "intra"), None),
            P("grp", "intra"),
            P(("intra", "grp"), None),
            P(("intra", "grp")),
            P(("intra", "grp")),
        ),
        check_vma=False,
    )
```

```python
import jax
import jax.numpy as jnp
from jax import lax
from jax.experimental import pallas as pl
from jax.experimental.pallas import tpu as pltpu
from jax.sharding import PartitionSpec as P

epsilon = 1e-05
F32, BF16 = jnp.float32, jnp.bfloat16
MESH = pl.DeviceIdType.MESH

T = 320
F = 1856
C = 512
H = 256
R = 29
SLOT = 32
OWN = 40
NI = 8
D = F * NI
COPIES = 140


def pack(v):
    tail = jnp.concatenate([v[32:40, :H], v[32:40, H:]], axis=0)
    return jnp.concatenate([v[0:16], v[16:32], tail], axis=1)


def unpack(v):
    tail = jnp.concatenate([v[0:8, 1024:], v[8:16, 1024:]], axis=1)
    return jnp.concatenate([v[:, :C], v[:, C:1024], tail], axis=0)


def iota(shape, dim):
    return lax.broadcasted_iota(jnp.int32, shape, dim)


def kernel(
    x_hbm, w_hbm, gain_hbm, bias_hbm, cot_hbm,
    proj_ref, ig_hbm, wg_ref, gg_ref, bg_ref,
    xv, w_ref, gain_ref, bias_ref, cot_ref, cv, igv, wfull, spread_m, squeeze_m,
    cot32, cotb, cotg, m32, wc, part32,
    gath, scat, land1, land2, scat2, land3, land4, scat3, land5, land6,
    st, stats1, stats2, cols, cols2, pown, pland,
    sends, recvs, local,
):
    grp, me = lax.axis_index("grp"), lax.axis_index("intra")
    z, y, x = grp // 16, (grp // 4) % 4, grp % 4
    core = me % 2

    def up(v, by):
        return (v + by) % 4

    def to_grp(axis, by):
        if axis == "z":
            return {"grp": up(z, by) * 16 + y * 4 + x, "intra": me}
        if axis == "y":
            return {"grp": z * 16 + up(y, by) * 4 + x, "intra": me}
        return {"grp": z * 16 + y * 4 + up(x, by), "intra": me}

    def to_intra(d):
        return {"grp": grp, "intra": (me + d) % NI}

    count = [0]

    def remote(src, dst, device):
        k = count[0]
        count[0] += 1
        return pltpu.make_async_remote_copy(
            src_ref=src, dst_ref=dst, send_sem=sends.at[k], recv_sem=recvs.at[k],
            device_id=device, device_id_type=MESH,
        )

    started = []

    def start(copies):
        for c in copies:
            c.start()
            started.append(c)
        return copies

    def arrive(copies):
        for c in copies:
            c.wait_recv()

    loads = [
        pltpu.make_async_copy(src, dst, local.at[k])
        for k, (src, dst) in enumerate((
            (w_hbm, w_ref), (gain_hbm, gain_ref), (bias_hbm, bias_ref), (cot_hbm, cot_ref), (x_hbm, xv),
        ))
    ]
    for load in loads:
        load.start()

    mate = {"grp": grp, "intra": me + 1 - 2 * core}
    peers = [to_grp(a, by) for a in "zyx" for by in (1, 3)] + [to_intra(d) for d in range(1, NI)]
    barrier = pltpu.get_barrier_semaphore()
    for peer in peers:
        pl.semaphore_signal(barrier, inc=1, device_id=peer, device_id_type=MESH)

    plane_of = (z, up(z, 3), up(z, 1), up(z, 2))
    groups = (slice(0, 1), slice(1, 3), slice(3, 4))

    for load in loads[:4]:
        load.wait()
    diagonal = iota((SLOT, R), 0) == iota((SLOT, R), 1)

    def column(ref):
        row = ref[...].astype(F32)
        return jnp.sum(jnp.where(diagonal, row, 0.0), axis=1, keepdims=True)

    gain, bias = column(gain_ref), column(bias_ref)
    wfull[...] = jnp.zeros_like(wfull)
    wfull[0:R, :] = w_ref[...].astype(F32)
    weight = wfull[...]
    product = jnp.sum(weight * bias, axis=0, keepdims=True)
    high = product.astype(BF16).astype(F32)
    row = iota((SLOT, C), 0)
    slot = jnp.where(row == R, high, jnp.where(row == R + 1, product - high, weight * gain)).astype(BF16)
    gath[0, 0, y, x] = slot[:, :H]
    gath[1, 0, y, x] = slot[:, H:]
    cotg[me] = pack(cot_ref[...].astype(F32)).astype(BF16)

    a, b = iota((H, 8 * R), 0), iota((H, 8 * R), 1)
    spread_m[...] = jnp.where(((a & 31) < R) & (b == R * (a >> 5) + (a & 31)), 1.0, 0.0).astype(BF16)
    a, b = iota((240, H), 0), iota((240, H), 1)
    within = b & 31
    hit = (within < R) & ((a == R * (b >> 5) + within) | (a == 233))
    hit = hit | ((within >= R) & (within < R + 2) & (a == 232))
    squeeze_m[...] = jnp.where(hit, 1.0, 0.0).astype(BF16)

    pl.semaphore_wait(barrier, len(peers))

    place = {"y": y, "x": x}
    whole, pairs, halves16 = slice(None), (slice(0, 2), slice(2, 4)), (slice(0, 16), slice(16, 32))

    def row_block(h, g, p, part):
        return gath.at[0, groups[g], p, x, part] if h == 0 else gath.at[1, groups[g], y, p, part]

    def plane_block(h, g, p, part):
        return gath.at[0, groups[g], part, p] if h == 0 else gath.at[1, groups[g], p, part]

    def ring_own(view, axes, g):
        copies = []
        for h in (0, 1):
            ref = view(h, g, place[axes[h]], whole)
            copies += [remote(ref, ref, to_grp(axes[h], by)) for by in (1, 3)]
        return start(copies)

    def ring_next(view, axes, parts, g, first):
        copies = []
        for h in (0, 1):
            p = place[axes[h]]
            arrive(first[2 * h:2 * h + 2])
            low, top = view(h, g, up(p, 3), parts[0]), view(h, g, up(p, 1), parts[1])
            copies += start([remote(low, low, to_grp(axes[h], 1)), remote(top, top, to_grp(axes[h], 3))])
        return copies

    def rows_own(g):
        return ring_own(row_block, "yx", g)

    def rows_next(g, first):
        return ring_next(row_block, "yx", halves16, g, first)

    def planes_own(g):
        return ring_own(plane_block, "xy", g)

    def planes_next(g, first):
        return ring_next(plane_block, "xy", pairs, g, first)

    gz1 = start([
        remote(gath.at[:, 0, y, x], gath.at[:, 1, y, x], to_grp("z", 1)),
        remote(gath.at[:, 0, y, x], gath.at[:, 2, y, x], to_grp("z", 3)),
    ])
    a0 = rows_own(0)
    ct1 = start([remote(cotg.at[me], cotg.at[me], mate)])
    ct1 += start([remote(cotg.at[me], cotg.at[me], to_intra(d)) for d in (2, 6, 4)])

    loads[4].wait()
    st[...] = jnp.zeros_like(st)
    lane = iota((64, 128), 1)
    for r in range(0, T, 64):
        v = xv[r:r + 64, :].astype(F32)
        s1 = jnp.sum(v, axis=1, keepdims=True)
        s2 = jnp.sum(v * v, axis=1, keepdims=True)
        st[r:r + 64, :] = jnp.where(lane == 0, s1, jnp.where(lane == 1, s2, 0.0))
    stats1[me] = st[...].T[0:2, :]
    ex1 = start([remote(stats1.at[me], stats1.at[me], to_intra(d)) for d in range(1, NI)])

    b0 = rows_next(0, a0)
    arrive(b0)
    c0 = planes_own(0)

    arrive(ex1)
    sums = jnp.sum(stats1[...], axis=0)
    average = sums[0:1] / D
    inverse = lax.rsqrt(sums[1:2] / D - average * average + epsilon)
    pick = iota((128, 384), 0)
    cols[...] = jnp.where(pick == 0, average, jnp.where(pick == 1, inverse, 0.0)).T
    for r in range(0, T, 64):
        v = xv[r:r + 64, :].astype(F32)
        cv[r:r + 64, :] = ((v - cols[r:r + 64, 0:1]) * cols[r:r + 64, 1:2]).astype(BF16)

    arrive(gz1)
    gz2 = start([
        remote(gath.at[0, 1, y, x], gath.at[0, 3, y, x], to_grp("z", 1)),
        remote(gath.at[1, 2, y, x], gath.at[1, 3, y, x], to_grp("z", 3)),
    ])
    a1 = rows_own(1)
    d0 = planes_next(0, c0)
    b1 = rows_next(1, a1)
    arrive(ct1)
    ct2 = start([remote(cotg.at[(me + d) % NI], cotg.at[(me + d) % NI], mate) for d in (6, 2, 4)])
    arrive(gz2)
    a2 = rows_own(2)
    arrive(b1)
    c1 = planes_own(1)
    b2 = rows_next(2, a2)

    arrive(ct2)
    for s in range(NI):
        cot32[OWN * s:OWN * s + OWN, :] = unpack(cotg[s].astype(F32))
    cotb[...] = cot32[...].astype(BF16)
    cot_sum = jnp.sum(cot32[...], axis=0, keepdims=True)

    arrive(b2)
    c2 = planes_own(2)

    for f in range(0, F, 256):
        g = min(f + 256, F)
        m32[f:g, :] = lax.dot_general(
            cv[:, f:g], cotb[...], (((0,), (0,)), ((), ())), preferred_element_type=F32
        )
    spare = (iota((H, C), 0) & 31) == R

    def spread(s):
        for j in range(2):
            base = pl.multiple_of(16 * R * plane_of[s] + 8 * R * j, 8)
            rows = m32[pl.ds(base, 8 * R), :].astype(BF16)
            wide = jnp.dot(spread_m[...], rows, preferred_element_type=F32)
            wide = jnp.where(spare, cot_sum, wide).astype(BF16)
            scat[0, s, 2 * j:2 * j + 2] = wide[:, :H].reshape(2, 4, SLOT, H)
            scat[1, s, 2 * j:2 * j + 2] = wide[:, H:].reshape(2, 4, SLOT, H)

    def plane_part(h, g, p, part):
        return scat.at[0, groups[g], part, p] if h == 0 else scat.at[1, groups[g], p, part]

    def row_part(h, g, p, part):
        return scat2.at[h, groups[g], p, part]

    def part_far(view, land, axes, parts, g):
        copies = []
        for h in (0, 1):
            far = up(place[axes[h]], 2)
            copies += [
                remote(view(h, g, far, parts[side]), land.at[h, side, groups[g]], to_grp(axes[h], by))
                for side, by in ((0, 1), (1, 3))
            ]
        return start(copies)

    def part_near(view, land, out, axes, parts, g, first):
        copies = []
        for h in (0, 1):
            arrive(first[2 * h:2 * h + 2])
            for side, by in ((0, 1), (1, 3)):
                near = up(place[axes[h]], by)
                ref = view(h, g, near, parts[side])
                ref[...] = (ref[...].astype(F32) + land[h, side, groups[g]].astype(F32)).astype(BF16)
                copies += start([remote(view(h, g, near, whole), out.at[h, side, groups[g]], to_grp(axes[h], by))])
        return copies

    def part_sum(view, out, axes, g, second, h):
        arrive(second[2 * h:2 * h + 2])
        total = view(h, g, place[axes[h]], whole)[...].astype(F32)
        return total + out[h, 0, groups[g]].astype(F32) + out[h, 1, groups[g]].astype(F32)

    def planes_far(g):
        return part_far(plane_part, land1, "xy", pairs, g)

    def planes_near(g, first):
        return part_near(plane_part, land1, land2, "xy", pairs, g, first)

    def planes_sum(g, second):
        for h in (0, 1):
            scat2[h, groups[g]] = part_sum(plane_part, land2, "xy", g, second, h).astype(BF16)

    def rows_far(g):
        return part_far(row_part, land3, "yx", halves16, g)

    def rows_near(g, first):
        return part_near(row_part, land3, land4, "yx", halves16, g, first)

    def rows_sum(g, second):
        for h in (0, 1):
            scat3[h, groups[g]] = part_sum(row_part, land4, "yx", g, second, h).astype(BF16)

    spread(3)
    e2 = planes_far(2)
    spread(1)
    spread(2)
    d1 = planes_next(1, c1)
    e1 = planes_far(1)
    spread(0)
    f2 = planes_near(2, e2)
    d2 = planes_next(2, c2)
    e0 = planes_far(0)

    extra = [jnp.zeros((8, H), F32), jnp.zeros((8, H), F32)]

    def squeeze(s):
        for h in (0, 1):
            block = gath[h, s].reshape(16 * SLOT, H)
            p0 = jnp.dot(squeeze_m[...], block[:H], preferred_element_type=F32)
            p1 = jnp.dot(squeeze_m[...], block[H:], preferred_element_type=F32)
            rows = jnp.concatenate([p0[:8 * R], p1[:8 * R]], axis=0)
            base = pl.multiple_of(16 * R * plane_of[s], 16)
            wc[pl.ds(base, 16 * R), H * h:H * (h + 1)] = rows.astype(BF16)
            extra[h] = extra[h] + p0[8 * R:] + p1[8 * R:]

    arrive(d0)
    squeeze(0)
    f1 = planes_near(1, e1)
    arrive(d1)
    squeeze(1)
    squeeze(2)
    planes_sum(2, f2)
    g2 = rows_far(2)
    arrive(d2)
    squeeze(3)
    extra = jnp.concatenate(extra, axis=1)
    bias_row, weight_row = extra[0:1], extra[1:2]
    f0 = planes_near(0, e0)

    part32[...] = jnp.dot(cv[...], wc[...], preferred_element_type=F32)
    cross = jnp.sum(cot32[...] * part32[...], axis=1, keepdims=True)
    plain = jnp.sum(cot32[...] * weight_row, axis=1, keepdims=True)
    lane = iota((T, 128), 1)
    st[0:T, :] = jnp.where(lane == 0, plain, jnp.where(lane == 1, cross, 0.0))
    stats2[me] = st[...].T[0:2, :]
    ex2 = start([remote(stats2.at[me], stats2.at[me], to_intra(d)) for d in range(1, NI)])
    h2 = rows_near(2, g2)
    for s in range(NI):
        pown[s] = pack(part32[OWN * s:OWN * s + OWN, :] + bias_row).astype(BF16)
    exp = start([remote(pown.at[(me + d) % NI], pland.at[d - 1], to_intra(d)) for d in range(1, NI)])

    planes_sum(1, f1)
    g1 = rows_far(1)
    rows_sum(2, h2)
    rz1 = start([
        remote(scat3.at[0, 3], land5.at[0], to_grp("z", 1)),
        remote(scat3.at[1, 3], land5.at[1], to_grp("z", 3)),
    ])

    arrive(ex2)
    means = jnp.sum(stats2[...], axis=0) / D
    cols2[...] = jnp.where(pick == 0, means[0:1], jnp.where(pick == 1, means[1:2], 0.0)).T

    def input_part(f):
        g = min(f + 256, F)
        scaled = lax.dot_general(
            cotb[...], wc[f:g, :], (((1,), (1,)), ((), ())), preferred_element_type=F32
        )
        centred = (xv[:, f:g].astype(F32) - cols[0:T, 0:1]) * cols[0:T, 1:2]
        value = cols[0:T, 1:2] * (scaled - cols2[0:T, 0:1] - centred * cols2[0:T, 1:2])
        igv[:, f:g] = value.astype(BF16)

    for f in range(0, 1024, 256):
        input_part(f)
    planes_sum(0, f0)
    g0 = rows_far(0)
    h1 = rows_near(1, g1)
    for f in range(1024, F, 256):
        input_part(f)
    ig_copy = pltpu.make_async_copy(igv, ig_hbm, local.at[0])
    ig_copy.start()

    h0 = rows_near(0, g0)
    rows_sum(1, h1)
    arrive(rz1)
    scat3[0, 2] = (scat3[0, 2].astype(F32) + land5[0].astype(F32)).astype(BF16)
    scat3[1, 1] = (scat3[1, 1].astype(F32) + land5[1].astype(F32)).astype(BF16)
    rz2 = start([
        remote(scat3.at[:, 2], land6.at[0], to_grp("z", 1)),
        remote(scat3.at[:, 1], land6.at[1], to_grp("z", 3)),
    ])

    arrive(exp)
    total = pown[me].astype(F32)
    for d in range(NI - 1):
        total = total + pland[d].astype(F32)
    proj_ref[...] = unpack(total).astype(BF16)

    mine = [part_sum(row_part, land4, "yx", 0, h0, h)[0] for h in (0, 1)]
    arrive(rz2)
    total = jnp.concatenate([
        mine[h] + land6[0, h].astype(F32) + land6[1, h].astype(F32) for h in (0, 1)
    ], axis=1)
    sum_row = total[R:R + 1]
    weight = wfull[...]
    wg_ref[...] = (total * gain + bias * sum_row)[:R]

    def as_row(v):
        return jnp.sum(jnp.where(diagonal, v, 0.0), axis=0, keepdims=True)

    gg_ref[...] = as_row(jnp.sum(weight * total, axis=1, keepdims=True))
    bg_ref[...] = as_row(jnp.sum(weight * sum_row, axis=1, keepdims=True))

    for c in started:
        c.wait_send()
    ig_copy.wait()


def writer(a, b, c, d, e, a_out, b_out, c_out, d_out, e_out, av, bv, cv, dv, ev, taken, given):
    tasks = [(b.at[r:r + 80], bv.at[r:r + 80], b_out.at[r:r + 80]) for r in range(0, T, 80)]
    tasks += [(a, av, a_out), (c, cv, c_out), (d, dv, d_out), (e, ev, e_out)]
    reads = [pltpu.make_async_copy(s, v, taken.at[k]) for k, (s, v, _) in enumerate(tasks)]
    writes = [pltpu.make_async_copy(v, o, given.at[k]) for k, (_, v, o) in enumerate(tasks)]
    for read in reads:
        read.start()
    for read, write in zip(reads, writes):
        read.wait()
        write.start()
    for write in writes:
        write.wait()


def shards(activations, norm_gain, norm_bias, kv_weight, kv_cotangent):
    vmem = pl.BlockSpec(memory_space=pltpu.VMEM)
    hbm = pl.BlockSpec(memory_space=pltpu.HBM)

    def v16(*shape):
        return pltpu.VMEM(shape, BF16)

    def v32(*shape):
        return pltpu.VMEM(shape, F32)

    shapes = (
        jax.ShapeDtypeStruct((OWN, C), BF16),
        jax.ShapeDtypeStruct((T, F), BF16),
        jax.ShapeDtypeStruct((R, C), F32),
        jax.ShapeDtypeStruct((1, R), F32),
        jax.ShapeDtypeStruct((1, R), F32),
    )
    results = pl.pallas_call(
        kernel,
        out_shape=shapes,
        in_specs=[hbm] * 5,
        out_specs=(vmem, hbm, vmem, vmem, vmem),
        scratch_shapes=[
            v16(T, F), v16(R, C), v16(1, R), v16(1, R), v16(OWN, C),
            v16(T, F), v16(T, F),
            v32(SLOT, C), v16(H, 8 * R), v16(240, H),
            v32(T, C), v16(T, C), v16(NI, 16, 1280), v32(F, C),
            v16(F, C), v32(T, C),
            v16(2, 4, 4, 4, SLOT, H), v16(2, 4, 4, 4, SLOT, H),
            v16(2, 2, 4, 2, SLOT, H), v16(2, 2, 4, 4, SLOT, H),
            v16(2, 4, 4, SLOT, H), v16(2, 2, 4, 16, H), v16(2, 2, 4, SLOT, H),
            v16(2, 4, SLOT, H), v16(2, SLOT, H), v16(2, 2, SLOT, H),
            v32(384, 128), v32(NI, 2, 384), v32(NI, 2, 384),
            v32(384, 128), v32(384, 128),
            v16(NI, 16, 1280), v16(NI - 1, 16, 1280),
            pltpu.SemaphoreType.DMA((COPIES,)),
            pltpu.SemaphoreType.DMA((COPIES,)),
            pltpu.SemaphoreType.DMA((5,)),
        ],
        compiler_params=pltpu.CompilerParams(
            collective_id=0, has_side_effects=True, vmem_limit_bytes=60 * 1024 * 1024
        ),
    )(activations, kv_weight, norm_gain.reshape(1, R), norm_bias.reshape(1, R), kv_cotangent)
    anywhere = pl.BlockSpec(memory_space=pl.ANY)
    projected, input_grad, weight_grad, gain_grad, bias_grad = pl.pallas_call(
        writer,
        out_shape=shapes,
        in_specs=[anywhere] * 5,
        out_specs=(hbm,) * 5,
        scratch_shapes=[
            v16(OWN, C), v16(T, F), v32(R, C), v32(1, R), v32(1, R),
            pltpu.SemaphoreType.DMA((8,)), pltpu.SemaphoreType.DMA((8,)),
        ],
        compiler_params=pltpu.CompilerParams(vmem_limit_bytes=60 * 1024 * 1024),
    )(*results)
    return projected, input_grad, weight_grad, gain_grad.reshape(R), bias_grad.reshape(R)


def solution(mesh):
    return jax.shard_map(
        shards,
        mesh=mesh,
        in_specs=(
            P("grp", "intra"),
            P(("intra", "grp")),
            P(("intra", "grp")),
            P(("intra", "grp"), None),
            P(("grp", "intra"), None),
        ),
        out_specs=(
            P(("grp", "intra"), None),
            P("grp", "intra"),
            P(("intra", "grp"), None),
            P(("intra", "grp")),
            P(("intra", "grp")),
        ),
        check_vma=False,
    )
```

```python
import jax
import jax.numpy as jnp
from jax import lax
from jax.experimental import pallas as pl
from jax.experimental.pallas import tpu as pltpu
from jax.sharding import PartitionSpec as P

epsilon = 1e-05
F32, BF16 = jnp.float32, jnp.bfloat16
MESH = pl.DeviceIdType.MESH

T = 320
F = 1856
C = 512
H = 256
R = 29
SLOT = 32
OWN = 40
NI = 8
D = F * NI
COPIES = 140
GATHER_DIRECT = (False, False, True)
SCATTER_DIRECT = (False, False, False)


def pack(v):
    tail = jnp.concatenate([v[32:40, :H], v[32:40, H:]], axis=0)
    return jnp.concatenate([v[0:16], v[16:32], tail], axis=1)


def unpack(v):
    tail = jnp.concatenate([v[0:8, 1024:], v[8:16, 1024:]], axis=1)
    return jnp.concatenate([v[:, :C], v[:, C:1024], tail], axis=0)


def iota(shape, dim):
    return lax.broadcasted_iota(jnp.int32, shape, dim)


def kernel(
    x_hbm, w_hbm, gain_hbm, bias_hbm, cot_hbm,
    proj_ref, ig_hbm, wg_ref, gg_ref, bg_ref,
    xv, w_ref, gain_ref, bias_ref, cot_ref, cv, igv, wfull, spread_m, squeeze_m,
    cot32, cotb, cotg, m32, wc, part32,
    gath, scat, land1, land2, scat2, land4, scat3, land5, land6,
    st, stats1, stats2, cols, cols2, pown, pmate, psum, pland,
    sends, recvs, local,
):
    grp, me = lax.axis_index("grp"), lax.axis_index("intra")
    z, y, x = grp // 16, (grp // 4) % 4, grp % 4
    core = me % 2

    def up(v, by):
        return (v + by) % 4

    def to_grp(axis, by):
        if axis == "z":
            return {"grp": up(z, by) * 16 + y * 4 + x, "intra": me}
        if axis == "y":
            return {"grp": z * 16 + up(y, by) * 4 + x, "intra": me}
        return {"grp": z * 16 + y * 4 + up(x, by), "intra": me}

    def to_intra(d):
        return {"grp": grp, "intra": (me + d) % NI}

    count = [0]

    def remote(src, dst, device):
        k = count[0]
        count[0] += 1
        return pltpu.make_async_remote_copy(
            src_ref=src, dst_ref=dst, send_sem=sends.at[k], recv_sem=recvs.at[k],
            device_id=device, device_id_type=MESH,
        )

    started = []

    def start(copies):
        for c in copies:
            c.start()
            started.append(c)
        return copies

    def drain(n):
        for c in started[:n]:
            c.wait_send()
        del started[:n]

    def arrive(copies):
        for c in copies:
            c.wait_recv()

    loads = [
        pltpu.make_async_copy(src, dst, local.at[k])
        for k, (src, dst) in enumerate((
            (w_hbm, w_ref), (gain_hbm, gain_ref), (bias_hbm, bias_ref), (cot_hbm, cot_ref), (x_hbm, xv),
        ))
    ]
    for load in loads:
        load.start()

    mate = {"grp": grp, "intra": me + 1 - 2 * core}
    peers = [to_grp(a, by) for a in "zyx" for by in (1, 2, 3)] + [to_intra(d) for d in range(1, NI)]
    barrier = pltpu.get_barrier_semaphore()
    for peer in peers:
        pl.semaphore_signal(barrier, inc=1, device_id=peer, device_id_type=MESH)

    plane_of = (z, up(z, 3), up(z, 1), up(z, 2))
    groups = (slice(0, 1), slice(1, 3), slice(3, 4))

    for load in loads[:3]:
        load.wait()
    diagonal = iota((SLOT, R), 0) == iota((SLOT, R), 1)

    def column(ref):
        row = ref[...].astype(F32)
        return jnp.sum(jnp.where(diagonal, row, 0.0), axis=1, keepdims=True)

    gain, bias = column(gain_ref), column(bias_ref)
    wfull[...] = jnp.zeros_like(wfull)
    wfull[0:R, :] = w_ref[...].astype(F32)
    weight = wfull[...]
    product = jnp.sum(weight * bias, axis=0, keepdims=True)
    high = product.astype(BF16).astype(F32)
    row = iota((SLOT, C), 0)
    slot = jnp.where(row == R, high, jnp.where(row == R + 1, product - high, weight * gain)).astype(BF16)
    gath[0, 0, y, x] = slot[:, :H]
    gath[1, 0, y, x] = slot[:, H:]

    pl.semaphore_wait(barrier, len(peers))

    place = {"y": y, "x": x}
    whole, pairs = slice(None), (slice(0, 2), slice(2, 4))

    def row_block(h, g, p, part):
        return gath.at[0, groups[g], p, x, part] if h == 0 else gath.at[1, groups[g], y, p, part]

    def plane_block(h, g, p, part):
        return gath.at[0, groups[g], part, p] if h == 0 else gath.at[1, groups[g], p, part]

    def ring_own(view, axes, g, direct):
        copies = []
        for h in (0, 1):
            ref = view(h, g, place[axes[h]], whole)
            copies += [remote(ref, ref, to_grp(axes[h], by)) for by in ((1, 3, 2) if direct else (1, 3))]
        return start(copies)

    def ring_next(view, axes, parts, g, first):
        copies = []
        for h in (0, 1):
            p = place[axes[h]]
            arrive(first[2 * h:2 * h + 2])
            low, top = view(h, g, up(p, 3), parts[0]), view(h, g, up(p, 1), parts[1])
            copies += start([remote(low, low, to_grp(axes[h], 1)), remote(top, top, to_grp(axes[h], 3))])
        return copies

    def rows_own(g):
        return ring_own(row_block, "yx", g, True)

    def planes_own(g):
        return ring_own(plane_block, "xy", g, GATHER_DIRECT[g])

    def planes_next(g, first):
        return first if GATHER_DIRECT[g] else ring_next(plane_block, "xy", pairs, g, first)

    def own_to(slot, by):
        return start([remote(gath.at[:, 0, y, x], gath.at[:, slot, y, x], to_grp("z", by))])

    gz1 = own_to(1, 1) + own_to(2, 3)
    a0 = rows_own(0)
    loads[3].wait()
    cotg[me] = pack(cot_ref[...].astype(F32)).astype(BF16)
    ct0 = start([remote(cotg.at[me], cotg.at[me], mate)])

    loads[4].wait()
    st[...] = jnp.zeros_like(st)
    lane = iota((64, 128), 1)
    for r in range(0, T, 64):
        v = xv[r:r + 64, :].astype(F32)
        s1 = jnp.sum(v, axis=1, keepdims=True)
        s2 = jnp.sum(v * v, axis=1, keepdims=True)
        st[r:r + 64, :] = jnp.where(lane == 0, s1, jnp.where(lane == 1, s2, 0.0))
    stats1[me] = st[...].T[0:2, :]
    ex1 = start([remote(stats1.at[me], stats1.at[me], to_intra(d)) for d in range(1, NI)])

    a, b = iota((H, 8 * R), 0), iota((H, 8 * R), 1)
    spread_m[...] = jnp.where(((a & 31) < R) & (b == R * (a >> 5) + (a & 31)), 1.0, 0.0).astype(BF16)
    a, b = iota((240, H), 0), iota((240, H), 1)
    within = b & 31
    hit = (within < R) & ((a == R * (b >> 5) + within) | (a == 233))
    hit = hit | ((within >= R) & (within < R + 2) & (a == 232))
    squeeze_m[...] = jnp.where(hit, 1.0, 0.0).astype(BF16)

    arrive(a0)
    c0 = planes_own(0)
    for c in gz1:
        c.wait_send()
    del started[:2]
    ct1 = start([remote(cotg.at[me], cotg.at[me], to_intra(d)) for d in (2, 6, 4)])

    arrive(ex1)
    sums = jnp.sum(stats1[...], axis=0)
    average = sums[0:1] / D
    inverse = lax.rsqrt(sums[1:2] / D - average * average + epsilon)
    pick = iota((128, 384), 0)
    cols[...] = jnp.where(pick == 0, average, jnp.where(pick == 1, inverse, 0.0)).T
    for r in range(0, T, 64):
        v = xv[r:r + 64, :].astype(F32)
        cv[r:r + 64, :] = ((v - cols[r:r + 64, 0:1]) * cols[r:r + 64, 1:2]).astype(BF16)

    arrive(gz1)
    gz2 = start([
        remote(gath.at[0, 1, y, x], gath.at[0, 3, y, x], to_grp("z", 1)),
        remote(gath.at[1, 2, y, x], gath.at[1, 3, y, x], to_grp("z", 3)),
    ])
    a1 = rows_own(1)
    d0 = planes_next(0, c0)
    arrive(a1)
    c1 = planes_own(1)
    arrive(ct1)
    ct2 = start([remote(cotg.at[(me + d) % NI], cotg.at[(me + d) % NI], mate) for d in (6, 2, 4)])
    arrive(gz2)
    a2 = rows_own(2)
    arrive(ct0)
    arrive(ct2)
    for s in range(NI):
        cot32[OWN * s:OWN * s + OWN, :] = unpack(cotg[s].astype(F32))
    cotb[...] = cot32[...].astype(BF16)
    cot_sum = jnp.sum(cot32[...], axis=0, keepdims=True)

    for f in range(0, F, 256):
        g = min(f + 256, F)
        m32[f:g, :] = lax.dot_general(
            cv[:, f:g], cotb[...], (((0,), (0,)), ((), ())), preferred_element_type=F32
        )
    spare = (iota((H, C), 0) & 31) == R

    def spread(s):
        for j in range(2):
            base = pl.multiple_of(16 * R * plane_of[s] + 8 * R * j, 8)
            rows = m32[pl.ds(base, 8 * R), :].astype(BF16)
            wide = jnp.dot(spread_m[...], rows, preferred_element_type=F32)
            wide = jnp.where(spare, cot_sum, wide).astype(BF16)
            scat[0, s, 2 * j:2 * j + 2] = wide[:, :H].reshape(2, 4, SLOT, H)
            scat[1, s, 2 * j:2 * j + 2] = wide[:, H:].reshape(2, 4, SLOT, H)

    def plane_part(h, g, p, part):
        return scat.at[0, groups[g], part, p] if h == 0 else scat.at[1, groups[g], p, part]

    def row_part(h, g, p, part):
        return scat2.at[h, groups[g], p, part]

    def part_far(view, land, out, axes, parts, g, direct):
        copies = []
        for h in (0, 1):
            p = place[axes[h]]
            if direct:
                copies += [
                    remote(view(h, g, up(p, by), whole), out.at[h, k, groups[g]], to_grp(axes[h], by))
                    for k, by in enumerate((1, 3, 2))
                ]
            else:
                copies += [
                    remote(view(h, g, up(p, 2), parts[k]), land.at[h, k, groups[g]], to_grp(axes[h], by))
                    for k, by in enumerate((1, 3))
                ]
        return start(copies)

    def part_near(view, land, out, axes, parts, g, first):
        copies = []
        for h in (0, 1):
            arrive(first[2 * h:2 * h + 2])
            for side, by in ((0, 1), (1, 3)):
                near = up(place[axes[h]], by)
                ref = view(h, g, near, parts[side])
                ref[...] = (ref[...].astype(F32) + land[h, side, groups[g]].astype(F32)).astype(BF16)
                copies += start([remote(view(h, g, near, whole), out.at[h, side, groups[g]], to_grp(axes[h], by))])
        return copies

    def part_sum(view, out, axes, g, last, h):
        n = len(last) // 2
        arrive(last[n * h:n * h + n])
        total = view(h, g, place[axes[h]], whole)[...].astype(F32)
        for k in range(n):
            total = total + out[h, k, groups[g]].astype(F32)
        return total

    def planes_far(g):
        return part_far(plane_part, land1, land2, "xy", pairs, g, SCATTER_DIRECT[g])

    def planes_near(g, first):
        return first if SCATTER_DIRECT[g] else part_near(plane_part, land1, land2, "xy", pairs, g, first)

    def planes_sum(g, last):
        for h in (0, 1):
            scat2[h, groups[g]] = part_sum(plane_part, land2, "xy", g, last, h).astype(BF16)

    def rows_far(g):
        return part_far(row_part, None, land4, "yx", None, g, True)

    def rows_sum(g, last):
        for h in (0, 1):
            scat3[h, groups[g]] = part_sum(row_part, land4, "yx", g, last, h).astype(BF16)

    def scatter_to(slot, by):
        return start([remote(scat3.at[:, slot], land6.at[slot - 1], to_grp("z", by))])

    spread(3)
    e2 = planes_far(2)
    arrive(a2)
    c2 = planes_own(2)
    spread(1)
    spread(2)
    e1 = planes_far(1)
    d1 = planes_next(1, c1)
    spread(0)
    f2 = planes_near(2, e2)
    drain(30)

    extra = [jnp.zeros((8, H), F32), jnp.zeros((8, H), F32)]

    def squeeze(s):
        for h in (0, 1):
            block = gath[h, s].reshape(16 * SLOT, H)
            p0 = jnp.dot(squeeze_m[...], block[:H], preferred_element_type=F32)
            p1 = jnp.dot(squeeze_m[...], block[H:], preferred_element_type=F32)
            rows = jnp.concatenate([p0[:8 * R], p1[:8 * R]], axis=0)
            base = pl.multiple_of(16 * R * plane_of[s], 16)
            wc[pl.ds(base, 16 * R), H * h:H * (h + 1)] = rows.astype(BF16)
            extra[h] = extra[h] + p0[8 * R:] + p1[8 * R:]

    arrive(d0)
    squeeze(0)
    d2 = planes_next(2, c2)
    f1 = planes_near(1, e1)
    e0 = planes_far(0)
    arrive(d1)
    squeeze(1)
    squeeze(2)
    planes_sum(2, f2)
    g2 = rows_far(2)
    arrive(d2)
    squeeze(3)
    extra = jnp.concatenate(extra, axis=1)
    bias_row, weight_row = extra[0:1], extra[1:2]

    part32[...] = jnp.dot(cv[...], wc[...], preferred_element_type=F32)
    cross = jnp.sum(cot32[...] * part32[...], axis=1, keepdims=True)
    plain = jnp.sum(cot32[...] * weight_row, axis=1, keepdims=True)
    lane = iota((T, 128), 1)
    st[0:T, :] = jnp.where(lane == 0, plain, jnp.where(lane == 1, cross, 0.0))
    stats2[me] = st[...].T[0:2, :]
    ex2 = start([remote(stats2.at[me], stats2.at[me], to_intra(d)) for d in range(1, NI)])
    def partial_rows(zl, c):
        base = pl.multiple_of(OWN * (2 * zl + c), 8)
        return pack(part32[pl.ds(base, OWN), :] + bias_row)

    for zl in range(4):
        pown[zl] = partial_rows(zl, 1 - core).astype(BF16)
    pair = start([remote(pown, pmate, mate)])
    f0 = planes_near(0, e0)
    rows_sum(2, g2)
    rz1 = start([
        remote(scat3.at[0, 3], land5.at[0], to_grp("z", 1)),
        remote(scat3.at[1, 3], land5.at[1], to_grp("z", 3)),
    ])
    arrive(pair)
    for zl in range(4):
        psum[zl] = (partial_rows(zl, core) + pmate[zl].astype(F32)).astype(BF16)
    exp = start([
        remote(psum.at[((me + d) % NI) // 2], pland.at[d // 2 - 1], to_intra(d)) for d in (2, 6, 4)
    ])

    planes_sum(1, f1)
    g1 = rows_far(1)

    arrive(ex2)
    means = jnp.sum(stats2[...], axis=0) / D
    cols2[...] = jnp.where(pick == 0, means[0:1], jnp.where(pick == 1, means[1:2], 0.0)).T

    def input_part(f):
        g = min(f + 256, F)
        scaled = lax.dot_general(
            cotb[...], wc[f:g, :], (((1,), (1,)), ((), ())), preferred_element_type=F32
        )
        centred = (xv[:, f:g].astype(F32) - cols[0:T, 0:1]) * cols[0:T, 1:2]
        value = cols[0:T, 1:2] * (scaled - cols2[0:T, 0:1] - centred * cols2[0:T, 1:2])
        igv[:, f:g] = value.astype(BF16)

    for f in range(0, 1024, 256):
        input_part(f)
    planes_sum(0, f0)
    g0 = rows_far(0)
    for f in range(1024, F, 256):
        input_part(f)
    ig_copy = pltpu.make_async_copy(igv, ig_hbm, local.at[0])
    ig_copy.start()

    drain(len(started) - 24)
    rows_sum(1, g1)
    arrive(rz1)
    scat3[0, 2] = (scat3[0, 2].astype(F32) + land5[0].astype(F32)).astype(BF16)
    scat3[1, 1] = (scat3[1, 1].astype(F32) + land5[1].astype(F32)).astype(BF16)
    rz2 = scatter_to(1, 3) + scatter_to(2, 1)

    arrive(exp)
    total = psum[me // 2].astype(F32)
    for d in range(3):
        total = total + pland[d].astype(F32)
    proj_ref[...] = unpack(total).astype(BF16)

    mine = [part_sum(row_part, land4, "yx", 0, g0, h)[0] for h in (0, 1)]
    arrive(rz2)
    for k in range(2):
        mine = [mine[h] + land6[k, h].astype(F32) for h in (0, 1)]
    total = jnp.concatenate(mine, axis=1)
    sum_row = total[R:R + 1]
    weight = wfull[...]
    wg_ref[...] = (total * gain + bias * sum_row)[:R]

    def as_row(v):
        return jnp.sum(jnp.where(diagonal, v, 0.0), axis=0, keepdims=True)

    gg_ref[...] = as_row(jnp.sum(weight * total, axis=1, keepdims=True))
    bg_ref[...] = as_row(jnp.sum(weight * sum_row, axis=1, keepdims=True))

    drain(len(started))
    ig_copy.wait()


def writer(a, b, c, d, e, a_out, b_out, c_out, d_out, e_out, av, bv, cv, dv, ev, taken, given):
    tasks = [(b.at[r:r + 80], bv.at[r:r + 80], b_out.at[r:r + 80]) for r in range(0, T, 80)]
    tasks += [(a, av, a_out), (c, cv, c_out), (d, dv, d_out), (e, ev, e_out)]
    reads = [pltpu.make_async_copy(s, v, taken.at[k]) for k, (s, v, _) in enumerate(tasks)]
    writes = [pltpu.make_async_copy(v, o, given.at[k]) for k, (_, v, o) in enumerate(tasks)]
    for read in reads:
        read.start()
    for read, write in zip(reads, writes):
        read.wait()
        write.start()
    for write in writes:
        write.wait()


def shards(activations, norm_gain, norm_bias, kv_weight, kv_cotangent):
    vmem = pl.BlockSpec(memory_space=pltpu.VMEM)
    hbm = pl.BlockSpec(memory_space=pltpu.HBM)

    def v16(*shape):
        return pltpu.VMEM(shape, BF16)

    def v32(*shape):
        return pltpu.VMEM(shape, F32)

    shapes = (
        jax.ShapeDtypeStruct((OWN, C), BF16),
        jax.ShapeDtypeStruct((T, F), BF16),
        jax.ShapeDtypeStruct((R, C), F32),
        jax.ShapeDtypeStruct((1, R), F32),
        jax.ShapeDtypeStruct((1, R), F32),
    )
    results = pl.pallas_call(
        kernel,
        out_shape=shapes,
        in_specs=[hbm] * 5,
        out_specs=(vmem, hbm, vmem, vmem, vmem),
        scratch_shapes=[
            v16(T, F), v16(R, C), v16(1, R), v16(1, R), v16(OWN, C),
            v16(T, F), v16(T, F),
            v32(SLOT, C), v16(H, 8 * R), v16(240, H),
            v32(T, C), v16(T, C), v16(NI, 16, 1280), v32(F, C),
            v16(F, C), v32(T, C),
            v16(2, 4, 4, 4, SLOT, H), v16(2, 4, 4, 4, SLOT, H),
            v16(2, 2, 4, 2, SLOT, H), v16(2, 3, 4, 4, SLOT, H),
            v16(2, 4, 4, SLOT, H), v16(2, 3, 4, SLOT, H),
            v16(2, 4, SLOT, H), v16(2, SLOT, H), v16(2, 2, SLOT, H),
            v32(384, 128), v32(NI, 2, 384), v32(NI, 2, 384),
            v32(384, 128), v32(384, 128),
            v16(4, 16, 1280), v16(4, 16, 1280), v16(4, 16, 1280), v16(3, 16, 1280),
            pltpu.SemaphoreType.DMA((COPIES,)),
            pltpu.SemaphoreType.DMA((COPIES,)),
            pltpu.SemaphoreType.DMA((5,)),
        ],
        compiler_params=pltpu.CompilerParams(
            collective_id=0, has_side_effects=True, vmem_limit_bytes=60 * 1024 * 1024
        ),
    )(activations, kv_weight, norm_gain.reshape(1, R), norm_bias.reshape(1, R), kv_cotangent)
    anywhere = pl.BlockSpec(memory_space=pl.ANY)
    projected, input_grad, weight_grad, gain_grad, bias_grad = pl.pallas_call(
        writer,
        out_shape=shapes,
        in_specs=[anywhere] * 5,
        out_specs=(hbm,) * 5,
        scratch_shapes=[
            v16(OWN, C), v16(T, F), v32(R, C), v32(1, R), v32(1, R),
            pltpu.SemaphoreType.DMA((8,)), pltpu.SemaphoreType.DMA((8,)),
        ],
        compiler_params=pltpu.CompilerParams(vmem_limit_bytes=60 * 1024 * 1024),
    )(*results)
    return projected, input_grad, weight_grad, gain_grad.reshape(R), bias_grad.reshape(R)


def solution(mesh):
    return jax.shard_map(
        shards,
        mesh=mesh,
        in_specs=(
            P("grp", "intra"),
            P(("intra", "grp")),
            P(("intra", "grp")),
            P(("intra", "grp"), None),
            P(("grp", "intra"), None),
        ),
        out_specs=(
            P(("grp", "intra"), None),
            P("grp", "intra"),
            P(("intra", "grp"), None),
            P(("intra", "grp")),
            P(("intra", "grp")),
        ),
        check_vma=False,
    )
```

```python
import jax
import jax.numpy as jnp
from jax import lax
from jax.experimental import pallas as pl
from jax.experimental.pallas import tpu as pltpu
from jax.sharding import PartitionSpec as P

epsilon = 1e-05
F32, BF16 = jnp.float32, jnp.bfloat16
MESH = pl.DeviceIdType.MESH

T = 320
F = 1856
C = 512
H = 256
R = 29
SLOT = 32
OWN = 40
NI = 8
D = F * NI
COPIES = 140
GATHER_DIRECT = (False, False, False)
SCATTER_DIRECT = (False, False, False)


def pack(v):
    tail = jnp.concatenate([v[32:40, :H], v[32:40, H:]], axis=0)
    return jnp.concatenate([v[0:16], v[16:32], tail], axis=1)


def unpack(v):
    tail = jnp.concatenate([v[0:8, 1024:], v[8:16, 1024:]], axis=1)
    return jnp.concatenate([v[:, :C], v[:, C:1024], tail], axis=0)


def iota(shape, dim):
    return lax.broadcasted_iota(jnp.int32, shape, dim)


def kernel(
    x_hbm, w_hbm, gain_hbm, bias_hbm, cot_hbm,
    proj_ref, ig_hbm, wg_ref, gg_ref, bg_ref,
    xv, w_ref, gain_ref, bias_ref, cot_ref, cv, igv, wfull, spread_m, squeeze_m,
    cot32, cotb, cotg, m32, wc, part32,
    gath, scat, land1, land2, scat2, land4, scat3, land5, land6,
    st, stats1, stats2, cols, cols2, pown, pmate, psum, pland,
    sends, recvs, local,
):
    grp, me = lax.axis_index("grp"), lax.axis_index("intra")
    z, y, x = grp // 16, (grp // 4) % 4, grp % 4
    core = me % 2

    def up(v, by):
        return (v + by) % 4

    def to_grp(axis, by):
        if axis == "z":
            return {"grp": up(z, by) * 16 + y * 4 + x, "intra": me}
        if axis == "y":
            return {"grp": z * 16 + up(y, by) * 4 + x, "intra": me}
        return {"grp": z * 16 + y * 4 + up(x, by), "intra": me}

    def to_intra(d):
        return {"grp": grp, "intra": (me + d) % NI}

    count = [0]

    def remote(src, dst, device):
        k = count[0]
        count[0] += 1
        return pltpu.make_async_remote_copy(
            src_ref=src, dst_ref=dst, send_sem=sends.at[k], recv_sem=recvs.at[k],
            device_id=device, device_id_type=MESH,
        )

    started = []

    def start(copies):
        for c in copies:
            c.start()
            started.append(c)
        return copies

    def drain(n):
        for c in started[:n]:
            c.wait_send()
        del started[:n]

    def arrive(copies):
        for c in copies:
            c.wait_recv()

    loads = [
        pltpu.make_async_copy(src, dst, local.at[k])
        for k, (src, dst) in enumerate((
            (w_hbm, w_ref), (gain_hbm, gain_ref), (bias_hbm, bias_ref), (cot_hbm, cot_ref), (x_hbm, xv),
        ))
    ]
    for load in loads:
        load.start()

    mate = {"grp": grp, "intra": me + 1 - 2 * core}
    peers = [to_grp(a, by) for a in "zyx" for by in (1, 2, 3)] + [to_intra(d) for d in range(1, NI)]
    barrier = pltpu.get_barrier_semaphore()
    for peer in peers:
        pl.semaphore_signal(barrier, inc=1, device_id=peer, device_id_type=MESH)

    plane_of = (z, up(z, 3), up(z, 1), up(z, 2))
    groups = (slice(0, 1), slice(1, 3), slice(3, 4))

    for load in loads[:3]:
        load.wait()
    diagonal = iota((SLOT, R), 0) == iota((SLOT, R), 1)

    def column(ref):
        row = ref[...].astype(F32)
        return jnp.sum(jnp.where(diagonal, row, 0.0), axis=1, keepdims=True)

    gain, bias = column(gain_ref), column(bias_ref)
    wfull[...] = jnp.zeros_like(wfull)
    wfull[0:R, :] = w_ref[...].astype(F32)
    weight = wfull[...]
    product = jnp.sum(weight * bias, axis=0, keepdims=True)
    high = product.astype(BF16).astype(F32)
    row = iota((SLOT, C), 0)
    slot = jnp.where(row == R, high, jnp.where(row == R + 1, product - high, weight * gain)).astype(BF16)
    gath[0, 0, y, x] = slot[:, :H]
    gath[1, 0, y, x] = slot[:, H:]

    pl.semaphore_wait(barrier, len(peers))

    place = {"y": y, "x": x}
    whole, pairs = slice(None), (slice(0, 2), slice(2, 4))

    def row_block(h, g, p, part):
        return gath.at[0, groups[g], p, x, part] if h == 0 else gath.at[1, groups[g], y, p, part]

    def plane_block(h, g, p, part):
        return gath.at[0, groups[g], part, p] if h == 0 else gath.at[1, groups[g], p, part]

    def ring_own(view, axes, g, direct):
        copies = []
        for h in (0, 1):
            ref = view(h, g, place[axes[h]], whole)
            copies += [remote(ref, ref, to_grp(axes[h], by)) for by in ((1, 3, 2) if direct else (1, 3))]
        return start(copies)

    def ring_next(view, axes, parts, g, first):
        copies = []
        for h in (0, 1):
            p = place[axes[h]]
            arrive(first[2 * h:2 * h + 2])
            low, top = view(h, g, up(p, 3), parts[0]), view(h, g, up(p, 1), parts[1])
            copies += start([remote(low, low, to_grp(axes[h], 1)), remote(top, top, to_grp(axes[h], 3))])
        return copies

    def rows_own(g):
        return ring_own(row_block, "yx", g, True)

    def planes_own(g):
        return ring_own(plane_block, "xy", g, GATHER_DIRECT[g])

    def planes_next(g, first):
        return first if GATHER_DIRECT[g] else ring_next(plane_block, "xy", pairs, g, first)

    def own_to(slot, by):
        return start([remote(gath.at[:, 0, y, x], gath.at[:, slot, y, x], to_grp("z", by))])

    gz1 = own_to(1, 1) + own_to(2, 3)
    a0 = rows_own(0)
    loads[3].wait()
    cotg[me] = pack(cot_ref[...].astype(F32)).astype(BF16)
    ct0 = start([remote(cotg.at[me], cotg.at[me], mate)])

    loads[4].wait()
    st[...] = jnp.zeros_like(st)
    lane = iota((64, 128), 1)
    for r in range(0, T, 64):
        v = xv[r:r + 64, :].astype(F32)
        s1 = jnp.sum(v, axis=1, keepdims=True)
        s2 = jnp.sum(v * v, axis=1, keepdims=True)
        st[r:r + 64, :] = jnp.where(lane == 0, s1, jnp.where(lane == 1, s2, 0.0))
    stats1[me] = st[...].T[0:2, :]
    ex1 = start([remote(stats1.at[me], stats1.at[me], to_intra(d)) for d in range(1, NI)])

    a, b = iota((H, 8 * R), 0), iota((H, 8 * R), 1)
    spread_m[...] = jnp.where(((a & 31) < R) & (b == R * (a >> 5) + (a & 31)), 1.0, 0.0).astype(BF16)
    a, b = iota((240, H), 0), iota((240, H), 1)
    within = b & 31
    hit = (within < R) & ((a == R * (b >> 5) + within) | (a == 233))
    hit = hit | ((within >= R) & (within < R + 2) & (a == 232))
    squeeze_m[...] = jnp.where(hit, 1.0, 0.0).astype(BF16)

    arrive(a0)
    c0 = planes_own(0)
    for c in gz1:
        c.wait_send()
    del started[:2]
    ct1 = start([remote(cotg.at[me], cotg.at[me], to_intra(d)) for d in (2, 6, 4)])

    arrive(ex1)
    sums = jnp.sum(stats1[...], axis=0)
    average = sums[0:1] / D
    inverse = lax.rsqrt(sums[1:2] / D - average * average + epsilon)
    pick = iota((128, 384), 0)
    cols[...] = jnp.where(pick == 0, average, jnp.where(pick == 1, inverse, 0.0)).T
    for r in range(0, T, 64):
        v = xv[r:r + 64, :].astype(F32)
        cv[r:r + 64, :] = ((v - cols[r:r + 64, 0:1]) * cols[r:r + 64, 1:2]).astype(BF16)

    arrive(gz1)
    gz2 = start([
        remote(gath.at[0, 1, y, x], gath.at[0, 3, y, x], to_grp("z", 1)),
        remote(gath.at[1, 2, y, x], gath.at[1, 3, y, x], to_grp("z", 3)),
    ])
    a1 = rows_own(1)
    d0 = planes_next(0, c0)
    arrive(a1)
    c1 = planes_own(1)
    arrive(ct1)
    ct2 = start([remote(cotg.at[(me + d) % NI], cotg.at[(me + d) % NI], mate) for d in (6, 2, 4)])
    arrive(gz2)
    a2 = rows_own(2)
    arrive(ct0)
    arrive(ct2)
    for s in range(NI):
        cot32[OWN * s:OWN * s + OWN, :] = unpack(cotg[s].astype(F32))
    cotb[...] = cot32[...].astype(BF16)
    cot_sum = jnp.sum(cot32[...], axis=0, keepdims=True)

    for f in range(0, F, 256):
        g = min(f + 256, F)
        m32[f:g, :] = lax.dot_general(
            cv[:, f:g], cotb[...], (((0,), (0,)), ((), ())), preferred_element_type=F32
        )
    spare = (iota((H, C), 0) & 31) == R

    def spread(s):
        for j in range(2):
            base = pl.multiple_of(16 * R * plane_of[s] + 8 * R * j, 8)
            rows = m32[pl.ds(base, 8 * R), :].astype(BF16)
            wide = jnp.dot(spread_m[...], rows, preferred_element_type=F32)
            wide = jnp.where(spare, cot_sum, wide).astype(BF16)
            scat[0, s, 2 * j:2 * j + 2] = wide[:, :H].reshape(2, 4, SLOT, H)
            scat[1, s, 2 * j:2 * j + 2] = wide[:, H:].reshape(2, 4, SLOT, H)

    def plane_part(h, g, p, part):
        return scat.at[0, groups[g], part, p] if h == 0 else scat.at[1, groups[g], p, part]

    def row_part(h, g, p, part):
        return scat2.at[h, groups[g], p, part]

    def part_far(view, land, out, axes, parts, g, direct):
        copies = []
        for h in (0, 1):
            p = place[axes[h]]
            if direct:
                copies += [
                    remote(view(h, g, up(p, by), whole), out.at[h, k, groups[g]], to_grp(axes[h], by))
                    for k, by in enumerate((1, 3, 2))
                ]
            else:
                copies += [
                    remote(view(h, g, up(p, 2), parts[k]), land.at[h, k, groups[g]], to_grp(axes[h], by))
                    for k, by in enumerate((1, 3))
                ]
        return start(copies)

    def part_near(view, land, out, axes, parts, g, first):
        copies = []
        for h in (0, 1):
            arrive(first[2 * h:2 * h + 2])
            for side, by in ((0, 1), (1, 3)):
                near = up(place[axes[h]], by)
                ref = view(h, g, near, parts[side])
                ref[...] = (ref[...].astype(F32) + land[h, side, groups[g]].astype(F32)).astype(BF16)
                copies += start([remote(view(h, g, near, whole), out.at[h, side, groups[g]], to_grp(axes[h], by))])
        return copies

    def part_sum(view, out, axes, g, last, h):
        n = len(last) // 2
        arrive(last[n * h:n * h + n])
        total = view(h, g, place[axes[h]], whole)[...].astype(F32)
        for k in range(n):
            total = total + out[h, k, groups[g]].astype(F32)
        return total

    def planes_far(g):
        return part_far(plane_part, land1, land2, "xy", pairs, g, SCATTER_DIRECT[g])

    def planes_near(g, first):
        return first if SCATTER_DIRECT[g] else part_near(plane_part, land1, land2, "xy", pairs, g, first)

    def planes_sum(g, last):
        for h in (0, 1):
            scat2[h, groups[g]] = part_sum(plane_part, land2, "xy", g, last, h).astype(BF16)

    def rows_far(g):
        return part_far(row_part, None, land4, "yx", None, g, True)

    def rows_sum(g, last):
        for h in (0, 1):
            scat3[h, groups[g]] = part_sum(row_part, land4, "yx", g, last, h).astype(BF16)

    def scatter_to(slot, by):
        return start([remote(scat3.at[:, slot], land6.at[slot - 1], to_grp("z", by))])

    spread(3)
    e2 = planes_far(2)
    arrive(a2)
    c2 = planes_own(2)
    spread(1)
    spread(2)
    e1 = planes_far(1)
    d1 = planes_next(1, c1)
    spread(0)
    f2 = planes_near(2, e2)
    drain(30)

    extra = [jnp.zeros((8, H), F32), jnp.zeros((8, H), F32)]

    def squeeze(s):
        for h in (0, 1):
            block = gath[h, s].reshape(16 * SLOT, H)
            p0 = jnp.dot(squeeze_m[...], block[:H], preferred_element_type=F32)
            p1 = jnp.dot(squeeze_m[...], block[H:], preferred_element_type=F32)
            rows = jnp.concatenate([p0[:8 * R], p1[:8 * R]], axis=0)
            base = pl.multiple_of(16 * R * plane_of[s], 16)
            wc[pl.ds(base, 16 * R), H * h:H * (h + 1)] = rows.astype(BF16)
            extra[h] = extra[h] + p0[8 * R:] + p1[8 * R:]

    arrive(d0)
    squeeze(0)
    d2 = planes_next(2, c2)
    f1 = planes_near(1, e1)
    e0 = planes_far(0)
    arrive(d1)
    squeeze(1)
    squeeze(2)
    planes_sum(2, f2)
    g2 = rows_far(2)
    arrive(d2)
    squeeze(3)
    extra = jnp.concatenate(extra, axis=1)
    bias_row, weight_row = extra[0:1], extra[1:2]

    part32[...] = jnp.dot(cv[...], wc[...], preferred_element_type=F32)
    cross = jnp.sum(cot32[...] * part32[...], axis=1, keepdims=True)
    plain = jnp.sum(cot32[...] * weight_row, axis=1, keepdims=True)
    lane = iota((T, 128), 1)
    st[0:T, :] = jnp.where(lane == 0, plain, jnp.where(lane == 1, cross, 0.0))
    stats2[me] = st[...].T[0:2, :]
    ex2 = start([remote(stats2.at[me], stats2.at[me], to_intra(d)) for d in range(1, NI)])
    def partial_rows(zl, c):
        base = pl.multiple_of(OWN * (2 * zl + c), 8)
        return pack(part32[pl.ds(base, OWN), :] + bias_row)

    for zl in range(4):
        pown[zl] = partial_rows(zl, 1 - core).astype(BF16)
    pair = start([remote(pown, pmate, mate)])
    f0 = planes_near(0, e0)
    rows_sum(2, g2)
    rz1 = start([
        remote(scat3.at[0, 3], land5.at[0], to_grp("z", 1)),
        remote(scat3.at[1, 3], land5.at[1], to_grp("z", 3)),
    ])
    arrive(pair)
    for zl in range(4):
        psum[zl] = (partial_rows(zl, core) + pmate[zl].astype(F32)).astype(BF16)
    exp = start([
        remote(psum.at[((me + d) % NI) // 2], pland.at[d // 2 - 1], to_intra(d)) for d in (2, 6, 4)
    ])

    planes_sum(1, f1)
    g1 = rows_far(1)

    arrive(ex2)
    means = jnp.sum(stats2[...], axis=0) / D
    cols2[...] = jnp.where(pick == 0, means[0:1], jnp.where(pick == 1, means[1:2], 0.0)).T

    def input_part(f):
        g = min(f + 256, F)
        scaled = lax.dot_general(
            cotb[...], wc[f:g, :], (((1,), (1,)), ((), ())), preferred_element_type=F32
        )
        centred = (xv[:, f:g].astype(F32) - cols[0:T, 0:1]) * cols[0:T, 1:2]
        value = cols[0:T, 1:2] * (scaled - cols2[0:T, 0:1] - centred * cols2[0:T, 1:2])
        igv[:, f:g] = value.astype(BF16)

    for f in range(0, 1024, 256):
        input_part(f)
    planes_sum(0, f0)
    g0 = rows_far(0)
    for f in range(1024, F, 256):
        input_part(f)
    ig_copy = pltpu.make_async_copy(igv, ig_hbm, local.at[0])
    ig_copy.start()

    drain(len(started) - 24)
    rows_sum(1, g1)
    arrive(rz1)
    scat3[0, 2] = (scat3[0, 2].astype(F32) + land5[0].astype(F32)).astype(BF16)
    scat3[1, 1] = (scat3[1, 1].astype(F32) + land5[1].astype(F32)).astype(BF16)
    rz2 = scatter_to(1, 3) + scatter_to(2, 1)

    arrive(exp)
    total = psum[me // 2].astype(F32)
    for d in range(3):
        total = total + pland[d].astype(F32)
    proj_ref[...] = unpack(total).astype(BF16)

    mine = [part_sum(row_part, land4, "yx", 0, g0, h)[0] for h in (0, 1)]
    arrive(rz2)
    for k in range(2):
        mine = [mine[h] + land6[k, h].astype(F32) for h in (0, 1)]
    total = jnp.concatenate(mine, axis=1)
    sum_row = total[R:R + 1]
    weight = wfull[...]
    wg_ref[...] = (total * gain + bias * sum_row)[:R]

    def as_row(v):
        return jnp.sum(jnp.where(diagonal, v, 0.0), axis=0, keepdims=True)

    gg_ref[...] = as_row(jnp.sum(weight * total, axis=1, keepdims=True))
    bg_ref[...] = as_row(jnp.sum(weight * sum_row, axis=1, keepdims=True))

    drain(len(started))
    ig_copy.wait()


def writer(a, b, c, d, e, a_out, b_out, c_out, d_out, e_out, av, bv, cv, dv, ev, taken, given):
    tasks = [(b.at[r:r + 80], bv.at[r:r + 80], b_out.at[r:r + 80]) for r in range(0, T, 80)]
    tasks += [(a, av, a_out), (c, cv, c_out), (d, dv, d_out), (e, ev, e_out)]
    reads = [pltpu.make_async_copy(s, v, taken.at[k]) for k, (s, v, _) in enumerate(tasks)]
    writes = [pltpu.make_async_copy(v, o, given.at[k]) for k, (_, v, o) in enumerate(tasks)]
    for read in reads:
        read.start()
    for read, write in zip(reads, writes):
        read.wait()
        write.start()
    for write in writes:
        write.wait()


def shards(activations, norm_gain, norm_bias, kv_weight, kv_cotangent):
    vmem = pl.BlockSpec(memory_space=pltpu.VMEM)
    hbm = pl.BlockSpec(memory_space=pltpu.HBM)

    def v16(*shape):
        return pltpu.VMEM(shape, BF16)

    def v32(*shape):
        return pltpu.VMEM(shape, F32)

    shapes = (
        jax.ShapeDtypeStruct((OWN, C), BF16),
        jax.ShapeDtypeStruct((T, F), BF16),
        jax.ShapeDtypeStruct((R, C), F32),
        jax.ShapeDtypeStruct((1, R), F32),
        jax.ShapeDtypeStruct((1, R), F32),
    )
    results = pl.pallas_call(
        kernel,
        out_shape=shapes,
        in_specs=[hbm] * 5,
        out_specs=(vmem, hbm, vmem, vmem, vmem),
        scratch_shapes=[
            v16(T, F), v16(R, C), v16(1, R), v16(1, R), v16(OWN, C),
            v16(T, F), v16(T, F),
            v32(SLOT, C), v16(H, 8 * R), v16(240, H),
            v32(T, C), v16(T, C), v16(NI, 16, 1280), v32(F, C),
            v16(F, C), v32(T, C),
            v16(2, 4, 4, 4, SLOT, H), v16(2, 4, 4, 4, SLOT, H),
            v16(2, 2, 4, 2, SLOT, H), v16(2, 3, 4, 4, SLOT, H),
            v16(2, 4, 4, SLOT, H), v16(2, 3, 4, SLOT, H),
            v16(2, 4, SLOT, H), v16(2, SLOT, H), v16(2, 2, SLOT, H),
            v32(384, 128), v32(NI, 2, 384), v32(NI, 2, 384),
            v32(384, 128), v32(384, 128),
            v16(4, 16, 1280), v16(4, 16, 1280), v16(4, 16, 1280), v16(3, 16, 1280),
            pltpu.SemaphoreType.DMA((COPIES,)),
            pltpu.SemaphoreType.DMA((COPIES,)),
            pltpu.SemaphoreType.DMA((5,)),
        ],
        compiler_params=pltpu.CompilerParams(
            collective_id=0, has_side_effects=True, vmem_limit_bytes=60 * 1024 * 1024
        ),
    )(activations, kv_weight, norm_gain.reshape(1, R), norm_bias.reshape(1, R), kv_cotangent)
    anywhere = pl.BlockSpec(memory_space=pl.ANY)
    projected, input_grad, weight_grad, gain_grad, bias_grad = pl.pallas_call(
        writer,
        out_shape=shapes,
        in_specs=[anywhere] * 5,
        out_specs=(hbm,) * 5,
        scratch_shapes=[
            v16(OWN, C), v16(T, F), v32(R, C), v32(1, R), v32(1, R),
            pltpu.SemaphoreType.DMA((8,)), pltpu.SemaphoreType.DMA((8,)),
        ],
        compiler_params=pltpu.CompilerParams(vmem_limit_bytes=60 * 1024 * 1024),
    )(*results)
    return projected, input_grad, weight_grad, gain_grad.reshape(R), bias_grad.reshape(R)


def solution(mesh):
    return jax.shard_map(
        shards,
        mesh=mesh,
        in_specs=(
            P("grp", "intra"),
            P(("intra", "grp")),
            P(("intra", "grp")),
            P(("intra", "grp"), None),
            P(("grp", "intra"), None),
        ),
        out_specs=(
            P(("grp", "intra"), None),
            P("grp", "intra"),
            P(("intra", "grp"), None),
            P(("intra", "grp")),
            P(("intra", "grp")),
        ),
        check_vma=False,
    )
```

```python
import jax
import jax.numpy as jnp
from jax import lax
from jax.experimental import pallas as pl
from jax.experimental.pallas import tpu as pltpu
from jax.sharding import PartitionSpec as P

epsilon = 1e-05
F32, BF16 = jnp.float32, jnp.bfloat16
MESH = pl.DeviceIdType.MESH

T = 320
F = 1856
C = 512
H = 256
R = 29
SLOT = 32
OWN = 40
NI = 8
D = F * NI
COPIES = 160
GATHER_DIRECT = (False, False, False, False)
SCATTER_DIRECT = (False, False, False, False)


def pack(v):
    tail = jnp.concatenate([v[32:40, :H], v[32:40, H:]], axis=0)
    return jnp.concatenate([v[0:16], v[16:32], tail], axis=1)


def unpack(v):
    tail = jnp.concatenate([v[0:8, 1024:], v[8:16, 1024:]], axis=1)
    return jnp.concatenate([v[:, :C], v[:, C:1024], tail], axis=0)


def iota(shape, dim):
    return lax.broadcasted_iota(jnp.int32, shape, dim)


def kernel(
    x_hbm, w_hbm, gain_hbm, bias_hbm, cot_hbm,
    proj_ref, ig_hbm, wg_ref, gg_ref, bg_ref,
    xv, w_ref, gain_ref, bias_ref, cot_ref, cv, igv, wfull, spread_m, squeeze_m,
    cot32, cotb, cotg, m32, wc, part32,
    gath, scat, land1, land2, scat2, land4, scat3, land5, land6,
    st, stats1, stats2, cols, cols2, pown, pmate, psum, pland,
    sends, recvs, local,
):
    grp, me = lax.axis_index("grp"), lax.axis_index("intra")
    z, y, x = grp // 16, (grp // 4) % 4, grp % 4
    core = me % 2

    def up(v, by):
        return (v + by) % 4

    def to_grp(axis, by):
        if axis == "z":
            return {"grp": up(z, by) * 16 + y * 4 + x, "intra": me}
        if axis == "y":
            return {"grp": z * 16 + up(y, by) * 4 + x, "intra": me}
        return {"grp": z * 16 + y * 4 + up(x, by), "intra": me}

    def to_intra(d):
        return {"grp": grp, "intra": (me + d) % NI}

    count = [0]

    def remote(src, dst, device):
        k = count[0]
        count[0] += 1
        return pltpu.make_async_remote_copy(
            src_ref=src, dst_ref=dst, send_sem=sends.at[k], recv_sem=recvs.at[k],
            device_id=device, device_id_type=MESH,
        )

    started = []

    def start(copies):
        for c in copies:
            c.start()
            started.append(c)
        return copies

    def drain(n):
        for c in started[:n]:
            c.wait_send()
        del started[:n]

    def arrive(copies):
        for c in copies:
            c.wait_recv()

    loads = [
        pltpu.make_async_copy(src, dst, local.at[k])
        for k, (src, dst) in enumerate((
            (w_hbm, w_ref), (gain_hbm, gain_ref), (bias_hbm, bias_ref), (cot_hbm, cot_ref), (x_hbm, xv),
        ))
    ]
    for load in loads:
        load.start()

    mate = {"grp": grp, "intra": me + 1 - 2 * core}
    peers = [to_grp(a, by) for a in "zyx" for by in (1, 2, 3)] + [to_intra(d) for d in range(1, NI)]
    barrier = pltpu.get_barrier_semaphore()
    for peer in peers:
        pl.semaphore_signal(barrier, inc=1, device_id=peer, device_id_type=MESH)

    plane_of = (z, up(z, 3), up(z, 1), up(z, 2))
    groups = tuple(slice(k, k + 1) for k in range(4))

    for load in loads[:3]:
        load.wait()
    diagonal = iota((SLOT, R), 0) == iota((SLOT, R), 1)

    def column(ref):
        row = ref[...].astype(F32)
        return jnp.sum(jnp.where(diagonal, row, 0.0), axis=1, keepdims=True)

    gain, bias = column(gain_ref), column(bias_ref)
    wfull[...] = jnp.zeros_like(wfull)
    wfull[0:R, :] = w_ref[...].astype(F32)
    weight = wfull[...]
    product = jnp.sum(weight * bias, axis=0, keepdims=True)
    high = product.astype(BF16).astype(F32)
    row = iota((SLOT, C), 0)
    slot = jnp.where(row == R, high, jnp.where(row == R + 1, product - high, weight * gain)).astype(BF16)
    gath[0, 0, y, x] = slot[:, :H]
    gath[1, 0, y, x] = slot[:, H:]

    pl.semaphore_wait(barrier, len(peers))

    place = {"y": y, "x": x}
    whole, pairs = slice(None), (slice(0, 2), slice(2, 4))

    def row_block(h, g, p, part):
        return gath.at[0, groups[g], p, x, part] if h == 0 else gath.at[1, groups[g], y, p, part]

    def plane_block(h, g, p, part):
        return gath.at[0, groups[g], part, p] if h == 0 else gath.at[1, groups[g], p, part]

    def ring_own(view, axes, g, direct):
        copies = []
        for h in (0, 1):
            ref = view(h, g, place[axes[h]], whole)
            copies += [remote(ref, ref, to_grp(axes[h], by)) for by in ((1, 3, 2) if direct else (1, 3))]
        return start(copies)

    def ring_next(view, axes, parts, g, first):
        copies = []
        for h in (0, 1):
            p = place[axes[h]]
            arrive(first[2 * h:2 * h + 2])
            low, top = view(h, g, up(p, 3), parts[0]), view(h, g, up(p, 1), parts[1])
            copies += start([remote(low, low, to_grp(axes[h], 1)), remote(top, top, to_grp(axes[h], 3))])
        return copies

    def rows_own(g):
        return ring_own(row_block, "yx", g, True)

    def planes_own(g):
        return ring_own(plane_block, "xy", g, GATHER_DIRECT[g])

    def planes_next(g, first):
        return first if GATHER_DIRECT[g] else ring_next(plane_block, "xy", pairs, g, first)

    def own_to(slot, by):
        return start([remote(gath.at[:, 0, y, x], gath.at[:, slot, y, x], to_grp("z", by))])

    gz1 = own_to(1, 1) + own_to(2, 3)
    a0 = rows_own(0)
    loads[3].wait()
    cotg[me] = pack(cot_ref[...].astype(F32)).astype(BF16)
    ct0 = start([remote(cotg.at[me], cotg.at[me], mate)])

    loads[4].wait()
    st[...] = jnp.zeros_like(st)
    lane = iota((64, 128), 1)
    for r in range(0, T, 64):
        v = xv[r:r + 64, :].astype(F32)
        s1 = jnp.sum(v, axis=1, keepdims=True)
        s2 = jnp.sum(v * v, axis=1, keepdims=True)
        st[r:r + 64, :] = jnp.where(lane == 0, s1, jnp.where(lane == 1, s2, 0.0))
    stats1[me] = st[...].T[0:2, :]
    ex1 = start([remote(stats1.at[me], stats1.at[me], to_intra(d)) for d in range(1, NI)])

    a, b = iota((H, 8 * R), 0), iota((H, 8 * R), 1)
    spread_m[...] = jnp.where(((a & 31) < R) & (b == R * (a >> 5) + (a & 31)), 1.0, 0.0).astype(BF16)
    a, b = iota((240, H), 0), iota((240, H), 1)
    within = b & 31
    hit = (within < R) & ((a == R * (b >> 5) + within) | (a == 233))
    hit = hit | ((within >= R) & (within < R + 2) & (a == 232))
    squeeze_m[...] = jnp.where(hit, 1.0, 0.0).astype(BF16)

    arrive(a0)
    c0 = planes_own(0)
    for c in gz1:
        c.wait_send()
    del started[:2]
    ct1 = start([remote(cotg.at[me], cotg.at[me], to_intra(d)) for d in (2, 6, 4)])

    arrive(ex1)
    sums = jnp.sum(stats1[...], axis=0)
    average = sums[0:1] / D
    inverse = lax.rsqrt(sums[1:2] / D - average * average + epsilon)
    pick = iota((128, 384), 0)
    cols[...] = jnp.where(pick == 0, average, jnp.where(pick == 1, inverse, 0.0)).T
    for r in range(0, T, 64):
        v = xv[r:r + 64, :].astype(F32)
        cv[r:r + 64, :] = ((v - cols[r:r + 64, 0:1]) * cols[r:r + 64, 1:2]).astype(BF16)

    arrive(gz1[:1])
    gz2 = start([remote(gath.at[0, 1, y, x], gath.at[0, 3, y, x], to_grp("z", 1))])
    a1 = rows_own(1)
    arrive(gz1[1:])
    gz2 += start([remote(gath.at[1, 2, y, x], gath.at[1, 3, y, x], to_grp("z", 3))])
    a2 = rows_own(2)
    d0 = planes_next(0, c0)
    arrive(a1)
    c1 = planes_own(1)
    arrive(a2)
    c2 = planes_own(2)
    arrive(ct1)
    ct2 = start([remote(cotg.at[(me + d) % NI], cotg.at[(me + d) % NI], mate) for d in (6, 2, 4)])
    arrive(gz2)
    a3 = rows_own(3)
    arrive(ct0)
    arrive(ct2)
    for s in range(NI):
        cot32[OWN * s:OWN * s + OWN, :] = unpack(cotg[s].astype(F32))
    cotb[...] = cot32[...].astype(BF16)
    cot_sum = jnp.sum(cot32[...], axis=0, keepdims=True)

    for f in range(0, F, 256):
        g = min(f + 256, F)
        m32[f:g, :] = lax.dot_general(
            cv[:, f:g], cotb[...], (((0,), (0,)), ((), ())), preferred_element_type=F32
        )
    spare = (iota((H, C), 0) & 31) == R

    def spread(s):
        for j in range(2):
            base = pl.multiple_of(16 * R * plane_of[s] + 8 * R * j, 8)
            rows = m32[pl.ds(base, 8 * R), :].astype(BF16)
            wide = jnp.dot(spread_m[...], rows, preferred_element_type=F32)
            wide = jnp.where(spare, cot_sum, wide).astype(BF16)
            scat[0, s, 2 * j:2 * j + 2] = wide[:, :H].reshape(2, 4, SLOT, H)
            scat[1, s, 2 * j:2 * j + 2] = wide[:, H:].reshape(2, 4, SLOT, H)

    def plane_part(h, g, p, part):
        return scat.at[0, groups[g], part, p] if h == 0 else scat.at[1, groups[g], p, part]

    def row_part(h, g, p, part):
        return scat2.at[h, groups[g], p, part]

    def part_far(view, land, out, axes, parts, g, direct):
        copies = []
        for h in (0, 1):
            p = place[axes[h]]
            if direct:
                copies += [
                    remote(view(h, g, up(p, by), whole), out.at[h, k, groups[g]], to_grp(axes[h], by))
                    for k, by in enumerate((1, 3, 2))
                ]
            else:
                copies += [
                    remote(view(h, g, up(p, 2), parts[k]), land.at[h, k, groups[g]], to_grp(axes[h], by))
                    for k, by in enumerate((1, 3))
                ]
        return start(copies)

    def part_near(view, land, out, axes, parts, g, first):
        copies = []
        for h in (0, 1):
            arrive(first[2 * h:2 * h + 2])
            for side, by in ((0, 1), (1, 3)):
                near = up(place[axes[h]], by)
                ref = view(h, g, near, parts[side])
                ref[...] = (ref[...].astype(F32) + land[h, side, groups[g]].astype(F32)).astype(BF16)
                copies += start([remote(view(h, g, near, whole), out.at[h, side, groups[g]], to_grp(axes[h], by))])
        return copies

    def part_sum(view, out, axes, g, last, h):
        n = len(last) // 2
        arrive(last[n * h:n * h + n])
        total = view(h, g, place[axes[h]], whole)[...].astype(F32)
        for k in range(n):
            total = total + out[h, k, groups[g]].astype(F32)
        return total

    def planes_far(g):
        return part_far(plane_part, land1, land2, "xy", pairs, g, SCATTER_DIRECT[g])

    def planes_near(g, first):
        return first if SCATTER_DIRECT[g] else part_near(plane_part, land1, land2, "xy", pairs, g, first)

    def planes_sum(g, last):
        for h in (0, 1):
            scat2[h, groups[g]] = part_sum(plane_part, land2, "xy", g, last, h).astype(BF16)

    def rows_far(g):
        return part_far(row_part, None, land4, "yx", None, g, True)

    def rows_sum(g, last):
        for h in (0, 1):
            scat3[h, groups[g]] = part_sum(row_part, land4, "yx", g, last, h).astype(BF16)

    def scatter_to(slot, by):
        return start([remote(scat3.at[:, slot], land6.at[slot - 1], to_grp("z", by))])

    spread(3)
    e3 = planes_far(3)
    arrive(a3)
    c3 = planes_own(3)
    spread(1)
    e1 = planes_far(1)
    d1 = planes_next(1, c1)
    spread(2)
    e2 = planes_far(2)
    d2 = planes_next(2, c2)
    spread(0)
    f3 = planes_near(3, e3)
    drain(30)

    extra = [jnp.zeros((8, H), F32), jnp.zeros((8, H), F32)]

    def squeeze(s):
        for h in (0, 1):
            block = gath[h, s].reshape(16 * SLOT, H)
            p0 = jnp.dot(squeeze_m[...], block[:H], preferred_element_type=F32)
            p1 = jnp.dot(squeeze_m[...], block[H:], preferred_element_type=F32)
            rows = jnp.concatenate([p0[:8 * R], p1[:8 * R]], axis=0)
            base = pl.multiple_of(16 * R * plane_of[s], 16)
            wc[pl.ds(base, 16 * R), H * h:H * (h + 1)] = rows.astype(BF16)
            extra[h] = extra[h] + p0[8 * R:] + p1[8 * R:]

    arrive(d0)
    squeeze(0)
    d3 = planes_next(3, c3)
    f1 = planes_near(1, e1)
    f2 = planes_near(2, e2)
    e0 = planes_far(0)
    arrive(d1)
    squeeze(1)
    arrive(d2)
    squeeze(2)
    planes_sum(3, f3)
    g3 = rows_far(3)
    arrive(d3)
    squeeze(3)
    extra = jnp.concatenate(extra, axis=1)
    bias_row, weight_row = extra[0:1], extra[1:2]

    part32[...] = jnp.dot(cv[...], wc[...], preferred_element_type=F32)
    cross = jnp.sum(cot32[...] * part32[...], axis=1, keepdims=True)
    plain = jnp.sum(cot32[...] * weight_row, axis=1, keepdims=True)
    lane = iota((T, 128), 1)
    st[0:T, :] = jnp.where(lane == 0, plain, jnp.where(lane == 1, cross, 0.0))
    stats2[me] = st[...].T[0:2, :]
    ex2 = start([remote(stats2.at[me], stats2.at[me], to_intra(d)) for d in range(1, NI)])
    def partial_rows(zl, c):
        base = pl.multiple_of(OWN * (2 * zl + c), 8)
        return pack(part32[pl.ds(base, OWN), :] + bias_row)

    for zl in range(4):
        pown[zl] = partial_rows(zl, 1 - core).astype(BF16)
    pair = start([remote(pown, pmate, mate)])
    f0 = planes_near(0, e0)
    rows_sum(3, g3)
    rz1 = start([
        remote(scat3.at[0, 3], land5.at[0], to_grp("z", 1)),
        remote(scat3.at[1, 3], land5.at[1], to_grp("z", 3)),
    ])
    arrive(pair)
    for zl in range(4):
        psum[zl] = (partial_rows(zl, core) + pmate[zl].astype(F32)).astype(BF16)
    exp = start([
        remote(psum.at[((me + d) % NI) // 2], pland.at[d // 2 - 1], to_intra(d)) for d in (2, 6, 4)
    ])

    planes_sum(1, f1)
    g1 = rows_far(1)
    planes_sum(2, f2)
    g2 = rows_far(2)

    arrive(ex2)
    means = jnp.sum(stats2[...], axis=0) / D
    cols2[...] = jnp.where(pick == 0, means[0:1], jnp.where(pick == 1, means[1:2], 0.0)).T

    def input_part(f):
        g = min(f + 256, F)
        scaled = lax.dot_general(
            cotb[...], wc[f:g, :], (((1,), (1,)), ((), ())), preferred_element_type=F32
        )
        centred = (xv[:, f:g].astype(F32) - cols[0:T, 0:1]) * cols[0:T, 1:2]
        value = cols[0:T, 1:2] * (scaled - cols2[0:T, 0:1] - centred * cols2[0:T, 1:2])
        igv[:, f:g] = value.astype(BF16)

    for f in range(0, 1024, 256):
        input_part(f)
    planes_sum(0, f0)
    g0 = rows_far(0)
    for f in range(1024, F, 256):
        input_part(f)
    ig_copy = pltpu.make_async_copy(igv, ig_hbm, local.at[0])
    ig_copy.start()

    drain(len(started) - 24)
    rows_sum(1, g1)
    arrive(rz1)
    scat3[1, 1] = (scat3[1, 1].astype(F32) + land5[1].astype(F32)).astype(BF16)
    rz2 = scatter_to(1, 3)
    rows_sum(2, g2)
    scat3[0, 2] = (scat3[0, 2].astype(F32) + land5[0].astype(F32)).astype(BF16)
    rz2 += scatter_to(2, 1)

    arrive(exp)
    total = psum[me // 2].astype(F32)
    for d in range(3):
        total = total + pland[d].astype(F32)
    proj_ref[...] = unpack(total).astype(BF16)

    mine = [part_sum(row_part, land4, "yx", 0, g0, h)[0] for h in (0, 1)]
    arrive(rz2)
    for k in range(2):
        mine = [mine[h] + land6[k, h].astype(F32) for h in (0, 1)]
    total = jnp.concatenate(mine, axis=1)
    sum_row = total[R:R + 1]
    weight = wfull[...]
    wg_ref[...] = (total * gain + bias * sum_row)[:R]

    def as_row(v):
        return jnp.sum(jnp.where(diagonal, v, 0.0), axis=0, keepdims=True)

    gg_ref[...] = as_row(jnp.sum(weight * total, axis=1, keepdims=True))
    bg_ref[...] = as_row(jnp.sum(weight * sum_row, axis=1, keepdims=True))

    drain(len(started))
    ig_copy.wait()


def writer(a, b, c, d, e, a_out, b_out, c_out, d_out, e_out, av, bv, cv, dv, ev, taken, given):
    tasks = [(b.at[r:r + 80], bv.at[r:r + 80], b_out.at[r:r + 80]) for r in range(0, T, 80)]
    tasks += [(a, av, a_out), (c, cv, c_out), (d, dv, d_out), (e, ev, e_out)]
    reads = [pltpu.make_async_copy(s, v, taken.at[k]) for k, (s, v, _) in enumerate(tasks)]
    writes = [pltpu.make_async_copy(v, o, given.at[k]) for k, (_, v, o) in enumerate(tasks)]
    for read in reads:
        read.start()
    for read, write in zip(reads, writes):
        read.wait()
        write.start()
    for write in writes:
        write.wait()


def shards(activations, norm_gain, norm_bias, kv_weight, kv_cotangent):
    vmem = pl.BlockSpec(memory_space=pltpu.VMEM)
    hbm = pl.BlockSpec(memory_space=pltpu.HBM)

    def v16(*shape):
        return pltpu.VMEM(shape, BF16)

    def v32(*shape):
        return pltpu.VMEM(shape, F32)

    shapes = (
        jax.ShapeDtypeStruct((OWN, C), BF16),
        jax.ShapeDtypeStruct((T, F), BF16),
        jax.ShapeDtypeStruct((R, C), F32),
        jax.ShapeDtypeStruct((1, R), F32),
        jax.ShapeDtypeStruct((1, R), F32),
    )
    results = pl.pallas_call(
        kernel,
        out_shape=shapes,
        in_specs=[hbm] * 5,
        out_specs=(vmem, hbm, vmem, vmem, vmem),
        scratch_shapes=[
            v16(T, F), v16(R, C), v16(1, R), v16(1, R), v16(OWN, C),
            v16(T, F), v16(T, F),
            v32(SLOT, C), v16(H, 8 * R), v16(240, H),
            v32(T, C), v16(T, C), v16(NI, 16, 1280), v32(F, C),
            v16(F, C), v32(T, C),
            v16(2, 4, 4, 4, SLOT, H), v16(2, 4, 4, 4, SLOT, H),
            v16(2, 2, 4, 2, SLOT, H), v16(2, 3, 4, 4, SLOT, H),
            v16(2, 4, 4, SLOT, H), v16(2, 3, 4, SLOT, H),
            v16(2, 4, SLOT, H), v16(2, SLOT, H), v16(2, 2, SLOT, H),
            v32(384, 128), v32(NI, 2, 384), v32(NI, 2, 384),
            v32(384, 128), v32(384, 128),
            v16(4, 16, 1280), v16(4, 16, 1280), v16(4, 16, 1280), v16(3, 16, 1280),
            pltpu.SemaphoreType.DMA((COPIES,)),
            pltpu.SemaphoreType.DMA((COPIES,)),
            pltpu.SemaphoreType.DMA((5,)),
        ],
        compiler_params=pltpu.CompilerParams(
            collective_id=0, has_side_effects=True, vmem_limit_bytes=60 * 1024 * 1024
        ),
    )(activations, kv_weight, norm_gain.reshape(1, R), norm_bias.reshape(1, R), kv_cotangent)
    anywhere = pl.BlockSpec(memory_space=pl.ANY)
    projected, input_grad, weight_grad, gain_grad, bias_grad = pl.pallas_call(
        writer,
        out_shape=shapes,
        in_specs=[anywhere] * 5,
        out_specs=(hbm,) * 5,
        scratch_shapes=[
            v16(OWN, C), v16(T, F), v32(R, C), v32(1, R), v32(1, R),
            pltpu.SemaphoreType.DMA((8,)), pltpu.SemaphoreType.DMA((8,)),
        ],
        compiler_params=pltpu.CompilerParams(vmem_limit_bytes=60 * 1024 * 1024),
    )(*results)
    return projected, input_grad, weight_grad, gain_grad.reshape(R), bias_grad.reshape(R)


def solution(mesh):
    return jax.shard_map(
        shards,
        mesh=mesh,
        in_specs=(
            P("grp", "intra"),
            P(("intra", "grp")),
            P(("intra", "grp")),
            P(("intra", "grp"), None),
            P(("grp", "intra"), None),
        ),
        out_specs=(
            P(("grp", "intra"), None),
            P("grp", "intra"),
            P(("intra", "grp"), None),
            P(("intra", "grp")),
            P(("intra", "grp")),
        ),
        check_vma=False,
    )
```
